32 devices in a mesh: groups: 2 (over x), ctx: 16 (over z, y, core).
Axes of the slice: x: 2, y: 2, z: 4, core: 2. Of those that a mesh axis runs over, the one named last changes fastest.
Arguments:
- queries: bfloat16 [4096, 1024], P(('groups', 'ctx')), parts along dimension 0, may hold values from -6 to 6
- keys: bfloat16 [4096, 1024], P(('groups', 'ctx')), parts along dimension 0, may hold values from -0.5 to 0.5
- values: bfloat16 [4096, 1024], P(('groups', 'ctx')), parts along dimension 0, may hold values from -6 to 6
- out_grad: bfloat16 [4096, 1024], P(('groups', 'ctx')), parts along dimension 0, may hold values from -0.059814453 to 0.059814453
- log_decay: bfloat16 [4096, 8], P(('groups', 'ctx')), parts along dimension 0, may hold values from -1 to 0
- frame_pos: int32 [4096], P(('groups', 'ctx')), parts along dimension 0, may hold values from 0 to 2047, as said below
- trial_lengths: int32 [16], P('groups'), parts along dimension 0, may hold values from 1 to 1024, 2048 in all
Outputs:
- query_grad: bfloat16 [4096, 1024], P(('groups', 'ctx')), parts along dimension 0
- key_grad: bfloat16 [4096, 1024], P(('groups', 'ctx')), parts along dimension 0
- value_grad: bfloat16 [4096, 1024], P(('groups', 'ctx')), parts along dimension 0
- decay_grad: bfloat16 [4096, 8], P(('groups', 'ctx')), parts along dimension 0
The draws below stay inside these ranges and needn't reach their ends.
There are 2 independent parts, one for each index of `groups`. The reference program is written for one: setup_inputs(seed, part) draws one part's arguments, and reference() takes and returns one part's arrays. A program takes and returns all parts, laid end to end along the dimension named above; each array names one. Nothing has to cross between parts.
Inputs may be any that keep to these rules, and one draw needn't show every extreme that they name: frame_pos is a permutation: the frame in loader row r sits at chain position frame_pos[r], and chain position p belongs to ctx index p // 128. The rows of one device bound for one device number at most 16, and exactly 16 for some pair of devices in every draw. `trial_lengths`: the lengths sum to 2048; the longest is exactly 1024; trials lie end to end in chain order.
All inputs are finite; a program needn't handle non-finite values.
Results may differ from the reference program's by a relative error of at most 0.0085.
Values may be sent and summed in bfloat16 or wider, within the bound.
No kernel may reach another device: no remote copies, remote signals or barrier semaphores. Data moves between devices by JAX's collectives and lax.ppermute only.
A program may use at most 192 MiB of HBM per device.

```python
import math
import jax
import jax.numpy as jnp
import numpy as np
from jax import lax

FOCUS_COUNT = 8
HEAD_DIM = 128
FR_DEV = 128
SPAN = 128
TRIALS = 8
SPAN_SNAPSHOTS = 2048
LONGEST = 1024
N_CTX = 16


def chain_positions(key):
    base_key = jax.random.fold_in(key, 101)
    lookup_tile_series = jax.random.split(base_key, 6)
    peer_count = N_CTX
    mean_rows = FR_DEV // N_CTX
    half_count = peer_count // 2
    shift_of = jax.random.permutation(lookup_tile_series[0], peer_count)
    relabel = jax.random.permutation(lookup_tile_series[1], peer_count)
    swing_rows = jax.random.randint(lookup_tile_series[2], (half_count,), -(mean_rows - 1), mean_rows)
    chosen = jax.random.randint(lookup_tile_series[3], (), 0, half_count)
    swing_rows = jnp.where(jnp.arange(half_count) == chosen, mean_rows, swing_rows)
    weights = jnp.concatenate([mean_rows + swing_rows, mean_rows - swing_rows]).astype(jnp.int32)
    weights = weights[jax.random.permutation(lookup_tile_series[4], peer_count)]
    bounds = jnp.cumsum(weights)
    slot_index = jnp.arange(FR_DEV, dtype=jnp.int32)
    group_id = jnp.sum((slot_index[:, None] >= bounds[None, :]).astype(jnp.int32), axis=1)
    owner_dev = relabel[(shift_of[:, None] + group_id[None, :]) % peer_count].reshape(-1)
    shuffle = jax.random.permutation(lookup_tile_series[5], SPAN_SNAPSHOTS)
    sorted_rows = shuffle[jnp.argsort(owner_dev[shuffle], stable=True)]
    return jnp.zeros((SPAN_SNAPSHOTS,), jnp.int32).at[sorted_rows].set(jnp.arange(SPAN_SNAPSHOTS, dtype=jnp.int32))


def draw_frame_pos(key, part):
    return chain_positions(key)


def draw_log_decay(key, part):
    linked_ordinal_slot = chain_positions(key)
    lookup_tile_series = jax.random.split(jax.random.fold_in(key, 202), 7)
    slow_share = 0.5
    slow_head = jax.random.uniform(lookup_tile_series[0], (FOCUS_COUNT,)) < slow_share
    slow_rate = jnp.exp(jax.random.uniform(lookup_tile_series[1], (FOCUS_COUNT,), minval=math.log(0.2 / SPAN_SNAPSHOTS), maxval=math.log(1.0 / SPAN_SNAPSHOTS)))
    fast_rate = jnp.exp(jax.random.uniform(lookup_tile_series[2], (FOCUS_COUNT,), minval=math.log(1.0 / 400.0), maxval=math.log(1.0 / 25.0)))
    channel_fading_speed = jnp.where(slow_head, slow_rate, fast_rate)
    device_scale = jnp.exp(jax.random.uniform(lookup_tile_series[3], (N_CTX,), minval=math.log(0.5), maxval=math.log(2.0)))
    snapshot_multiplier = device_scale[linked_ordinal_slot // FR_DEV]
    stochastic_jitter = jax.random.uniform(lookup_tile_series[4], (SPAN_SNAPSHOTS, FOCUS_COUNT), minval=0.5, maxval=1.5)
    spurt_opening_snapshot = jax.random.randint(lookup_tile_series[5], (4,), 0, SPAN_SNAPSHOTS)
    within_spurt_flags = jnp.any(linked_ordinal_slot[:, None] == spurt_opening_snapshot[None, :], axis=1)
    spurt_fading_objective = jax.random.uniform(lookup_tile_series[6], (SPAN_SNAPSHOTS, FOCUS_COUNT), minval=math.log(0.5), maxval=math.log(0.8))
    fading_result_lines = -channel_fading_speed[None, :] * snapshot_multiplier[:, None] * stochastic_jitter + jnp.where(within_spurt_flags[:, None], spurt_fading_objective, 0.0)
    return fading_result_lines.astype(jnp.bfloat16)


def steps_of(stream_key, extent, pieces, least, top_value):
    def one(axis_at, parts):
        draws = jax.random.uniform(jax.random.fold_in(jax.random.fold_in(stream_key, 6), axis_at), (parts,), jnp.float32, least / len(pieces), top_value / len(pieces))
        return jnp.repeat(jnp.exp(draws), extent[axis_at] // parts).reshape((-1,) + (1,) * (len(extent) - axis_at - 1))

    gain = one(*pieces[0])
    for cut in pieces[1:]:
        gain = gain * one(*cut)
    return gain


def split_up(count, total, limit, lean):
    weights = [(1 << 20) // math.isqrt(grade ** lean) + 1 for grade in range(2, count + 1)]
    rest, holding = total - limit - (count - 1), [1] * (count - 1)
    while rest > 0:
        movable = [i for i in range(count - 1) if holding[i] < limit]
        pool, left = sum([weights[i] for i in movable]), rest
        for i in movable:
            more = min(limit - holding[i], max(1, left * weights[i] // pool), rest)
            holding[i] = holding[i] + more
            rest = rest - more
    return np.array([limit] + holding)


def uneven_parts(stream_key, number_of, total, most, lean):
    if number_of == 2:
        one = jax.random.randint(stream_key, (), max(1, total - most), min(most, total - 1) + 1)
        return jnp.stack([one, total - one])
    sizes = jnp.asarray(split_up(number_of, total, most, lean), jnp.int32)
    couples = (number_of - 1) // 2
    donor, receiver = sizes[1:1 + 2 * couples:2], sizes[2:2 + 2 * couples:2]
    room = jnp.minimum(donor - 1, most - receiver)
    passed = jax.random.randint(jax.random.fold_in(stream_key, 1), (couples,), 0, 1 << 20) % (room + 1)
    sizes = sizes.at[1:1 + 2 * couples:2].set(donor - passed).at[2:2 + 2 * couples:2].set(receiver + passed)
    return sizes[jax.random.permutation(jax.random.fold_in(stream_key, 2), number_of)]


def normal_values(rng, shape, width, limit, cuts=(), kind=jnp.bfloat16):
    array = jax.random.normal(rng, shape, jnp.float32) * width
    if len(cuts) > 0:
        array = steps_of(rng, shape, cuts, -0.22, 0.18) * array
    return jnp.clip(array, min=-limit, max=limit).astype(kind)


def setup_inputs(seed: int = 0, part: int = 0) -> dict:
    streams_of = jax.random.split(jax.random.key(seed), 8)
    part_splits = jax.random.split(jax.random.fold_in(streams_of[7], part), 8)
    queries = normal_values(part_splits[0], (SPAN_SNAPSHOTS, FOCUS_COUNT * HEAD_DIM), 1.0, 6.0, ((0, 16),))
    keys = normal_values(part_splits[1], (SPAN_SNAPSHOTS, FOCUS_COUNT * HEAD_DIM), HEAD_DIM ** -0.5, 0.5, ((0, 16),))
    values = normal_values(part_splits[2], (SPAN_SNAPSHOTS, FOCUS_COUNT * HEAD_DIM), 1.0, 6.0, ((0, 16),))
    out_grad = normal_values(part_splits[3], (SPAN_SNAPSHOTS, FOCUS_COUNT * HEAD_DIM), 0.01, 0.059814453, ((0, 16),))
    log_decay = draw_log_decay(jax.random.fold_in(jax.random.fold_in(streams_of[7], part), 71), part)
    frame_pos = draw_frame_pos(jax.random.fold_in(jax.random.fold_in(streams_of[7], part), 71), part)
    trial_lengths = uneven_parts(part_splits[6], TRIALS, SPAN_SNAPSHOTS, LONGEST, 1).astype(jnp.int32)
    return dict(queries=queries, keys=keys, values=values, out_grad=out_grad, log_decay=log_decay, frame_pos=frame_pos, trial_lengths=trial_lengths)


def product(form, left, right):
    return jnp.einsum(form, left.astype(jnp.float32), right.astype(jnp.float32), precision=lax.Precision.HIGHEST)


def block_gains(cum_decay, start_marks):
    query_gain = jnp.where(start_marks[:, None] == 0, jnp.exp(cum_decay), 0.0)
    key_gain = jnp.where(start_marks[:, None] == start_marks[-1], jnp.exp(cum_decay[-1][None, :] - cum_decay), 0.0)
    span_fade = jnp.where(start_marks[-1] == 0, jnp.exp(cum_decay[-1]), 0.0)
    return query_gain, key_gain, span_fade


def span_summary(query_block, key_block, value_block, grad_block, cum_decay, start_marks):
    query_gain, key_gain, span_fade = block_gains(cum_decay, start_marks)
    key_end = (key_block.astype(jnp.float32) * key_gain[:, :, None]).astype(jnp.bfloat16)
    query_start = (query_block.astype(jnp.float32) * query_gain[:, :, None]).astype(jnp.bfloat16)
    carried = product("jhd,jhe->hde", key_end, value_block)
    pulled = product("ihd,ihe->hde", query_start, grad_block)
    return carried, pulled, span_fade


def span_grads(query_block, key_block, value_block, grad_block, cum_decay, start_marks, state_low, grad_low):
    query_gain, key_gain, span_fade = block_gains(cum_decay, start_marks)
    block_size = query_block.shape[0]
    lower_tri = jnp.arange(block_size)[:, None] >= jnp.arange(block_size)[None, :]
    keep_pair = (lower_tri & (start_marks[:, None] == start_marks[None, :]))[None]
    decay_head = cum_decay.T
    decay_gap = decay_head[:, :, None] - decay_head[:, None, :]
    weight = jnp.where(keep_pair, jnp.exp(jnp.where(keep_pair, decay_gap, 0.0)), 0.0)
    scores = product("ihd,jhd->hij", query_block, key_block)
    grad_score = product("ihe,jhe->hij", grad_block, value_block)
    score_weighted = (scores * weight).astype(jnp.bfloat16)
    grad_weighted = (grad_score * weight).astype(jnp.bfloat16)
    query_grad = product("hij,jhd->ihd", grad_weighted, key_block) + query_gain[:, :, None] * product("ihe,hde->ihd", grad_block, state_low)
    key_grad = product("hij,ihd->jhd", grad_weighted, query_block) + key_gain[:, :, None] * product("jhe,hde->jhd", value_block, grad_low)
    value_grad = product("hij,ihe->jhe", score_weighted, grad_block) + key_gain[:, :, None] * product("jhd,hde->jhe", key_block, grad_low)
    decay_term = jnp.sum(query_block.astype(jnp.float32) * query_grad - key_block.astype(jnp.float32) * key_grad, axis=2)
    return query_grad, key_grad, value_grad, decay_term


def reference(queries, keys, values, out_grad, log_decay, frame_pos, trial_lengths):
    frame_count = queries.shape[0]
    block_count = frame_count // SPAN

    def to_chain(source):
        return jnp.zeros_like(source).at[frame_pos].set(source)

    def chain_blocks(source):
        return to_chain(source).reshape(block_count, SPAN, FOCUS_COUNT, HEAD_DIM)

    query_chain = chain_blocks(queries)
    key_chain = chain_blocks(keys)
    value_chain = chain_blocks(values)
    grad_chain = chain_blocks(out_grad)
    cum_decay = jnp.cumsum(to_chain(log_decay).astype(jnp.float32).reshape(block_count, SPAN, FOCUS_COUNT), axis=1)
    position = jnp.arange(frame_count, dtype=jnp.int32)
    starts = (jnp.cumsum(trial_lengths) - trial_lengths).astype(jnp.int32)
    is_start = jnp.any(position[:, None] == starts[None, :], axis=1)
    start_marks = jnp.cumsum(is_start.reshape(block_count, SPAN).astype(jnp.int32), axis=1)
    carried, pulled, span_fade = lax.map(lambda packed: span_summary(*packed), (query_chain, key_chain, value_chain, grad_chain, cum_decay, start_marks))

    def forward(state_now, item_pair):
        added, factor = item_pair
        return factor[:, None, None] * state_now + added, state_now

    empty_state = jnp.zeros((FOCUS_COUNT, HEAD_DIM, HEAD_DIM), jnp.float32)
    _, state_in = lax.scan(forward, empty_state, (carried, span_fade))
    _, grad_end = lax.scan(forward, empty_state, (pulled, span_fade), reverse=True)
    query_grad, key_grad, value_grad, decay_term = lax.map(
        lambda packed: span_grads(*packed),
        (query_chain, key_chain, value_chain, grad_chain, cum_decay, start_marks, state_in.astype(jnp.bfloat16), grad_end.astype(jnp.bfloat16)))
    decay_term = decay_term.reshape(frame_count, FOCUS_COUNT)
    follows = jnp.concatenate([is_start[1:], jnp.ones((1,), dtype=bool)])

    def backward(running, item_set):
        term_now, cut_here, start_here = item_set
        summed = term_now + jnp.where(cut_here, 0.0, running)
        return summed, jnp.where(start_here, 0.0, summed)

    _, tail_grad = lax.scan(backward, jnp.zeros((FOCUS_COUNT,), jnp.float32), (decay_term, follows, is_start), reverse=True)

    def to_loader(source):
        return source.reshape(frame_count, -1)[frame_pos].astype(jnp.bfloat16)

    return (to_loader(query_grad), to_loader(key_grad), to_loader(value_grad), to_loader(tail_grad))
```

```python
import functools

import jax
import jax.numpy as jnp
from jax import lax
from jax.experimental import pallas as pl
from jax.experimental.pallas import tpu as pltpu
from jax.sharding import PartitionSpec as P

SPAN = 128
META = 16
F32 = jnp.float32
BF16 = jnp.bfloat16
I32 = jnp.int32
VMEM = pl.BlockSpec(memory_space=pltpu.VMEM)
SMEM = pl.BlockSpec(memory_space=pltpu.SMEM)


def dot(a, b, dims):
    return lax.dot_general(a, b, ((dims[:1], dims[1:]), ((), ())), preferred_element_type=F32)


NN = (1, 0)
NT = (1, 1)
TN = (0, 0)


def iota(shape, dim):
    return lax.broadcasted_iota(I32, shape, dim)


def pack_kernel(chip_ref, q_ref, k_ref, v_ref, g_ref, ld_ref, pos_ref, *outs):
    rows = q_ref.shape[0]
    heads = len(outs)
    chip = chip_ref[0]
    eye = (iota((META, heads), 0) == iota((META, heads), 1)).astype(BF16)
    decay = dot(eye, ld_ref[...], NT)
    pos = pos_ref[...]
    line = iota((META, rows), 0)
    tail = jnp.where(line == 1, (pos // SPAN).astype(F32), jnp.where(line == 2, (pos % SPAN).astype(F32), 0.0))
    for s in range(heads):
        head = chip ^ s
        at = pl.ds(pl.multiple_of(head * SPAN, SPAN), SPAN)
        for n, ref in enumerate((q_ref, k_ref, v_ref, g_ref)):
            outs[s][n * rows:(n + 1) * rows, :] = ref[:, at]
        mine = jnp.sum(jnp.where(line == head, decay, 0.0), axis=0, keepdims=True)
        outs[s][4 * rows:, :] = jnp.where(line == 0, mine, tail).astype(BF16)


def segments(position, starts):
    total = jnp.zeros_like(position)
    for start in starts:
        total = total + (position >= start).astype(I32)
    return total


def chain_kernel(heads, lengths_ref, *refs):
    sources = len(refs) - heads - 12
    blocks, outs, scratch = refs[:sources], refs[sources:sources + heads], refs[sources + heads:]
    (x_ref, hi_ref, lo_ref, cum_ref, chain_ref, gained_ref, weighted_ref,
     carried_ref, pulled_ref, state_ref, grad_ref, tail_ref) = scratch
    rows = (blocks[0].shape[0] - META) // 4
    frames = rows * sources
    spans = frames // SPAN
    starts = []
    total = jnp.int32(0)
    for t in range(lengths_ref.shape[0]):
        starts.append(total)
        total = total + lengths_ref[t]

    for n, ref in enumerate(blocks):
        for a in range(4):
            x_ref[n * rows:(n + 1) * rows, a * SPAN:(a + 1) * SPAN] = ref[a * rows:(a + 1) * rows, :]
        meta = ref[4 * rows:, :].astype(F32)
        hi_ref[:, n * rows:(n + 1) * rows] = meta[1:2].astype(I32)
        lo_ref[:, n * rows:(n + 1) * rows] = meta[2:3].astype(I32)
    decay_parts = [ref[4 * rows:, :].astype(F32)[0:1] for ref in blocks]
    decay = jnp.concatenate(decay_parts, axis=1)
    hi = hi_ref[...]
    lo = lo_ref[...]
    pad = cum_ref.shape[0]
    spread = jnp.where(hi == iota((pad, frames), 0), decay, 0.0).astype(BF16)
    where_lo = (lo == iota((SPAN, frames), 0)).astype(BF16)
    in_chain = dot(spread, where_lo, NT).astype(BF16)
    upper = (iota((SPAN, SPAN), 0) <= iota((SPAN, SPAN), 1)).astype(BF16)
    cum_ref[...] = dot(in_chain, upper, NN)
    tail_ref[...] = jnp.zeros_like(tail_ref)

    row_i = iota((SPAN, SPAN), 0)
    col_j = iota((SPAN, SPAN), 1)

    def first(b):
        base = b * SPAN
        at = pl.ds(pl.multiple_of(base, SPAN), SPAN)
        key = jnp.where(hi_ref[...] == b, lo_ref[...], -1)
        hot = (key == iota((SPAN, frames), 0)).astype(BF16)
        chain = dot(hot, x_ref[...], NN).astype(BF16)
        chain_ref[at, :] = chain
        q, k, v, g = (chain[:, a * SPAN:(a + 1) * SPAN] for a in range(4))
        cum_j = cum_ref[pl.ds(b, 1), :]
        cum_i = jnp.transpose(jnp.broadcast_to(cum_j, (SPAN, SPAN)))
        last = cum_j[:, SPAN - 1:]
        seg_i = segments(base + row_i, starts)
        seg_j = segments(base + iota((1, SPAN), 1), starts)
        before = segments(jnp.full((1, 1), base - 1, I32), starts)
        end = segments(jnp.full((1, 1), base + SPAN - 1, I32), starts)
        same = seg_i == seg_j
        gap = cum_i - cum_j
        lower = same & (row_i >= col_j)
        higher = same & (row_i <= col_j)
        weight = jnp.where(lower, jnp.exp(jnp.where(lower, gap, 0.0)), 0.0)
        weight_t = jnp.where(higher, jnp.exp(jnp.where(higher, -gap, 0.0)), 0.0)
        query_gain = jnp.where(seg_i == before, jnp.exp(cum_i), 0.0)
        key_gain = jnp.where(seg_i == end, jnp.exp(last - cum_i), 0.0)
        key_end = (k.astype(F32) * key_gain).astype(BF16)
        query_start = (q.astype(F32) * query_gain).astype(BF16)
        gained_ref[at, 0:SPAN] = (g.astype(F32) * query_gain).astype(BF16)
        gained_ref[at, SPAN:2 * SPAN] = (v.astype(F32) * key_gain).astype(BF16)
        gained_ref[at, 2 * SPAN:] = key_end
        carried_ref[at, :] = dot(key_end, v, TN)
        pulled_ref[at, :] = dot(query_start, g, TN)
        weighted_ref[at, 0:SPAN] = (dot(g, v, NT) * weight).astype(BF16)
        weighted_ref[at, SPAN:2 * SPAN] = (dot(v, g, NT) * weight_t).astype(BF16)
        weighted_ref[at, 2 * SPAN:] = (dot(k, q, NT) * weight_t).astype(BF16)

    def second(b):
        base = b * SPAN
        at = pl.ds(pl.multiple_of(base, SPAN), SPAN)
        q, k, v, g = (chain_ref[at, a * SPAN:(a + 1) * SPAN] for a in range(4))
        state = state_ref[at, :]
        grad = grad_ref[at, :]
        dq = dot(weighted_ref[at, 0:SPAN], k, NN) + dot(gained_ref[at, 0:SPAN], state, NT)
        dk = dot(weighted_ref[at, SPAN:2 * SPAN], q, NN) + dot(gained_ref[at, SPAN:2 * SPAN], grad, NT)
        dv = dot(weighted_ref[at, 2 * SPAN:], g, NN) + dot(gained_ref[at, 2 * SPAN:], grad, NN)
        term = jnp.sum(q.astype(F32) * dq - k.astype(F32) * dk, axis=1, keepdims=True)
        seg_i = segments(base + row_i, starts)
        seg_j = segments(base + iota((1, SPAN), 1), starts)
        lower = (seg_i == seg_j) & (row_i >= col_j)
        tail_ref[pl.ds(b, 1), :] = jnp.sum(jnp.where(lower, term, 0.0), axis=0, keepdims=True)
        chain_ref[at, 0:SPAN] = dq.astype(BF16)
        chain_ref[at, SPAN:2 * SPAN] = dk.astype(BF16)
        chain_ref[at, 2 * SPAN:3 * SPAN] = dv.astype(BF16)

    step = 4 if spans % 4 == 0 else 1

    @pl.loop(0, spans // step)
    def _(turn):
        for u in range(step):
            first(turn * step + u)

    def fade(b):
        last = cum_ref[pl.ds(b, 1), SPAN - 1:]
        before = segments(jnp.full((1, 1), b * SPAN - 1, I32), starts)
        end = segments(jnp.full((1, 1), b * SPAN + SPAN - 1, I32), starts)
        return jnp.where(before == end, jnp.exp(last), 0.0)

    def scan(turn, held):
        state, grad = held
        b, c = turn, spans - 1 - turn
        at_b = pl.ds(pl.multiple_of(b * SPAN, SPAN), SPAN)
        at_c = pl.ds(pl.multiple_of(c * SPAN, SPAN), SPAN)
        state_ref[at_b, :] = state.astype(BF16)
        grad_ref[at_c, :] = grad.astype(BF16)
        return fade(b) * state + carried_ref[at_b, :], fade(c) * grad + pulled_ref[at_c, :]

    empty = jnp.zeros((SPAN, SPAN), F32)
    lax.fori_loop(0, spans, scan, (empty, empty))

    @pl.loop(0, spans // step)
    def _(turn):
        for u in range(step):
            second(turn * step + u)

    local = tail_ref[...]
    firsts = jnp.transpose(local)[0:1, :]
    seg_last = segments(row_i * SPAN + SPAN - 1, starts)
    seg_first = segments(col_j * SPAN, starts)
    later = (col_j > row_i) & (seg_first == seg_last)
    carry = jnp.sum(jnp.where(later, firsts, 0.0), axis=1, keepdims=True)
    place = row_i * SPAN + col_j
    full = local + jnp.where(segments(place, starts) == seg_last, carry, 0.0)
    begins = place == starts[0]
    for start in starts[1:]:
        begins = begins | (place == start)
    tails = jnp.where(begins, 0.0, full).astype(BF16)

    wanted = hi_ref[:, :heads * rows] * SPAN + lo_ref[:, :heads * rows]
    for s in range(heads):
        part = slice(s * rows, (s + 1) * rows)
        where_row = jnp.broadcast_to(wanted[:, part].astype(F32), (SPAN, rows))
        where_col = jnp.transpose(where_row)[:, 0:1].astype(I32)
        hot = (where_col == iota((rows, frames), 1)).astype(BF16)
        back = dot(hot, chain_ref[:, 0:3 * SPAN], NN).astype(BF16)
        for a in range(3):
            outs[s][a * rows:(a + 1) * rows, :] = back[:, a * SPAN:(a + 1) * SPAN]
        hot_lo = (lo_ref[:, part] == iota((SPAN, rows), 0)).astype(BF16)
        found = dot(tails, hot_lo, NN)
        found = jnp.sum(jnp.where(hi_ref[:, part] == iota((SPAN, rows), 0), found, 0.0), axis=0, keepdims=True)
        outs[s][3 * rows:, :] = jnp.broadcast_to(found, (META, rows)).astype(BF16)


def unpack_kernel(chip_ref, *refs):
    heads = len(refs) - 4
    blocks, outs = refs[:heads], refs[heads:]
    rows = outs[0].shape[0]
    chip = chip_ref[0]
    line = iota((SPAN, rows), 0)
    tails = jnp.zeros((SPAN, rows), F32)
    for s in range(heads):
        head = chip ^ s
        at = pl.ds(pl.multiple_of(head * SPAN, SPAN), SPAN)
        for a in range(3):
            outs[a][:, at] = blocks[s][a * rows:(a + 1) * rows, :]
        tails = jnp.where(line == head, blocks[s][3 * rows:, :].astype(F32)[0:1], tails)
    outs[3][...] = jnp.transpose(tails)[:, :heads].astype(BF16)


def body(queries, keys, values, out_grad, log_decay, frame_pos, trial_lengths):
    rows, width = queries.shape
    heads = log_decay.shape[1]
    peers = lax.axis_size("ctx")
    cores = peers // heads
    frames = rows * peers
    spans = frames // SPAN
    chip = (lax.axis_index("ctx") // cores).astype(I32).reshape(1)

    def across(x, s):
        return lax.ppermute(x, "ctx", [(p, p ^ (s * cores)) for p in range(peers)])

    def beside(x, t):
        return lax.ppermute(x, "ctx", [(p, p ^ t) for p in range(peers)])

    packets = pl.pallas_call(
        pack_kernel,
        out_shape=[jax.ShapeDtypeStruct((4 * rows + META, SPAN), BF16)] * heads,
        in_specs=[SMEM] + [VMEM] * 6,
        out_specs=[VMEM] * heads,
        name="pack",
    )(chip, queries, keys, values, out_grad, log_decay, frame_pos.reshape(1, rows))
    got = list(packets)
    for s in (6, 7, 4, 5, 2, 3, 1):
        got[s] = across(packets[s], s)
    everything = list(got)
    for t in range(1, cores):
        everything += [beside(x, t) for x in got]

    tall = max(SPAN, spans)
    back = pl.pallas_call(
        functools.partial(chain_kernel, heads),
        out_shape=[jax.ShapeDtypeStruct((3 * rows + META, SPAN), BF16)] * heads,
        in_specs=[SMEM] + [VMEM] * peers,
        out_specs=[VMEM] * heads,
        scratch_shapes=[
            pltpu.VMEM((frames, 4 * SPAN), BF16),
            pltpu.VMEM((1, frames), I32),
            pltpu.VMEM((1, frames), I32),
            pltpu.VMEM((tall, SPAN), F32),
            pltpu.VMEM((frames, 4 * SPAN), BF16),
            pltpu.VMEM((frames, 3 * SPAN), BF16),
            pltpu.VMEM((frames, 3 * SPAN), BF16),
            pltpu.VMEM((frames, SPAN), F32),
            pltpu.VMEM((frames, SPAN), F32),
            pltpu.VMEM((frames, SPAN), BF16),
            pltpu.VMEM((frames, SPAN), BF16),
            pltpu.VMEM((tall, SPAN), F32),
        ],
        compiler_params=pltpu.CompilerParams(vmem_limit_bytes=60 * 2**20),
        name="chain",
    )(trial_lengths, *everything)
    returned = list(back)
    for s in (6, 7, 4, 5, 2, 3, 1):
        returned[s] = across(back[s], s)

    return tuple(pl.pallas_call(
        unpack_kernel,
        out_shape=[jax.ShapeDtypeStruct((rows, width), BF16)] * 3 + [jax.ShapeDtypeStruct((rows, heads), BF16)],
        in_specs=[SMEM] + [VMEM] * heads,
        out_specs=[VMEM] * 4,
        name="unpack",
    )(chip, *returned))


def solution(mesh):
    rows = P(("groups", "ctx"), None)
    return jax.shard_map(
        body,
        mesh=mesh,
        in_specs=(rows, rows, rows, rows, rows, P(("groups", "ctx")), P("groups")),
        out_specs=(rows, rows, rows, rows),
        check_vma=False,
    )
```

```python
import functools

import jax
import jax.numpy as jnp
from jax import lax
from jax.experimental import pallas as pl
from jax.experimental.pallas import tpu as pltpu
from jax.sharding import PartitionSpec as P

SPAN = 128
META = 16
F32 = jnp.float32
BF16 = jnp.bfloat16
I32 = jnp.int32
VMEM = pl.BlockSpec(memory_space=pltpu.VMEM)
SMEM = pl.BlockSpec(memory_space=pltpu.SMEM)


def dot(a, b, dims):
    return lax.dot_general(a, b, ((dims[:1], dims[1:]), ((), ())), preferred_element_type=F32)


NN = (1, 0)
NT = (1, 1)
TN = (0, 0)


def iota(shape, dim):
    return lax.broadcasted_iota(I32, shape, dim)


def order(pos):
    rows = pos.shape[1]
    across = jnp.broadcast_to(pos.astype(F32), (rows, rows))
    down = jnp.transpose(across)
    as_row = jnp.sum((down < across).astype(F32), axis=0, keepdims=True)
    as_col = jnp.sum((across < down).astype(F32), axis=1, keepdims=True)
    return as_row.astype(I32), as_col.astype(I32)


def pack_kernel(chip_ref, q_ref, k_ref, v_ref, g_ref, ld_ref, pos_ref, *outs):
    rows = q_ref.shape[0]
    heads = len(outs)
    chip = chip_ref[0]
    pos = pos_ref[...]
    rank, _ = order(pos)
    sort = (rank == iota((rows, rows), 0)).astype(BF16)
    for s in range(heads):
        head = chip ^ ((heads - s) % heads)
        at = pl.ds(pl.multiple_of(head * SPAN, SPAN), SPAN)
        together = jnp.concatenate([ref[:, at] for ref in (q_ref, k_ref, v_ref, g_ref)], axis=1)
        together = dot(sort, together, NN).astype(BF16)
        for a in range(4):
            outs[s][a * rows:(a + 1) * rows, :] = together[:, a * SPAN:(a + 1) * SPAN]
    line = iota((META, rows), 0)
    where = jnp.where(line == 1, (pos // SPAN).astype(F32), jnp.where(line == 2, (pos % SPAN + 1).astype(F32), 0.0))
    where = dot(where.astype(BF16), sort, NT)
    decay = dot(ld_ref[...], sort, NT)
    for s in range(heads):
        head = chip ^ ((heads - s) % heads)
        mine = jnp.sum(jnp.where(iota((heads, rows), 0) == head, decay, 0.0), axis=0, keepdims=True)
        outs[s][4 * rows:, :] = jnp.where(line == 0, mine, where).astype(BF16)


def segments(position, starts):
    total = jnp.zeros_like(position)
    for start in starts:
        total = total + (position >= start).astype(I32)
    return total


def chain_kernel(heads, lengths_ref, *refs):
    sources = len(refs) - heads - 14
    blocks, outs, scratch = refs[:sources], refs[sources:sources + heads], refs[sources + heads:]
    (hi_ref, lo_ref, win_ref, at_ref, sem, key_ref, cum_ref, chain_ref, gained_ref, weighted_ref,
     carried_ref, pulled_ref, low_ref, tail_ref) = scratch
    rows = (blocks[0].shape[0] - META) // 4
    frames = rows * sources
    spans = frames // SPAN
    window = 16 * pl.cdiv(2 * rows // sources, 16) + 16
    tall = cum_ref.shape[0]
    starts = []
    total = jnp.int32(0)
    for t in range(lengths_ref.shape[0]):
        starts.append(total)
        total = total + lengths_ref[t]

    for n, ref in enumerate(blocks):
        meta = ref[4 * rows:, :].astype(F32)
        hi_ref[n:n + 1, :] = meta[1:2]
        lo_ref[n:n + 1, :] = meta[2:3]
    hi = hi_ref[...]
    lane = iota((sources, SPAN), 1)
    count = jnp.zeros((sources, SPAN), F32)
    for b in range(1, spans):
        ahead = jnp.sum((hi < b).astype(F32), axis=1, keepdims=True)
        count = jnp.where(lane == b, ahead, count)
    win_ref[...] = jnp.minimum((count.astype(I32) // 16) * 16, rows - window)
    copy = pltpu.make_async_copy(win_ref, at_ref, sem)
    copy.start()

    spread = []
    hots = []
    for n, ref in enumerate(blocks):
        meta = ref[4 * rows:, :].astype(F32)
        spread.append(jnp.where(meta[1:2] == iota((tall, rows), 0).astype(F32), meta[0:1], 0.0).astype(BF16))
        hots.append((meta[2:3] == (iota((SPAN, rows), 0) + 1).astype(F32)).astype(BF16))
    in_chain = dot(jnp.concatenate(spread, axis=1), jnp.concatenate(hots, axis=1), NT).astype(BF16)
    upper = (iota((SPAN, SPAN), 0) <= iota((SPAN, SPAN), 1)).astype(BF16)
    place = iota((tall, SPAN), 0) * SPAN + iota((tall, SPAN), 1)
    marks = segments(place, starts) - segments(iota((tall, SPAN), 0) * SPAN - 1, starts)
    cum_ref[...] = dot(in_chain, upper, NN) - 128.0 * marks.astype(F32)
    tail_ref[...] = jnp.zeros_like(tail_ref)
    for ref in outs:
        ref[...] = jnp.zeros_like(ref)

    row_i = iota((SPAN, SPAN), 0)
    col_j = iota((SPAN, SPAN), 1)
    per = SPAN // window
    copy.wait()

    def first(b):
        base = b * SPAN
        at = pl.ds(pl.multiple_of(base, SPAN), SPAN)
        keys = jnp.where(hi_ref[...] == b.astype(F32), lo_ref[...], 0.0)
        chain = jnp.zeros((SPAN, 4 * SPAN), F32)
        for n0 in range(0, sources, 2 * per):
            parts, found = [], []
            for n1 in range(n0, n0 + 2 * per, per):
                row = None
                for n in range(n1, n1 + per):
                    begin = pl.multiple_of(at_ref[n, b], 16)
                    turned = pltpu.roll(keys[n:n + 1], (n - n1) * window + SPAN - begin, 1)
                    row = turned if row is None else row + turned
                    found.append(jnp.concatenate(
                        [blocks[n][pl.ds(a * rows + begin, window), :] for a in range(4)], axis=1))
                parts.append(row)
            row = jnp.concatenate(parts, axis=1)
            key_ref[pl.ds(b, 1), n0 * window:(n0 + 2 * per) * window] = row
            hot = (row == (iota((SPAN, 2 * per * window), 0) + 1).astype(F32)).astype(BF16)
            chain = chain + dot(hot, jnp.concatenate(found, axis=0), NN)
        chain = chain.astype(BF16)
        chain_ref[at, :] = chain
        q, k, v, g = (chain[:, a * SPAN:(a + 1) * SPAN] for a in range(4))
        cum_j = cum_ref[pl.ds(b, 1), :]
        cum_i = jnp.transpose(jnp.broadcast_to(cum_j, (SPAN, SPAN)))
        last = cum_j[:, SPAN - 1:]
        gap = cum_i - cum_j
        weight = jnp.where(row_i >= col_j, jnp.exp(jnp.minimum(gap, 0.0)), 0.0)
        weight_t = jnp.where(row_i <= col_j, jnp.exp(jnp.minimum(-gap, 0.0)), 0.0)
        query_gain = jnp.exp(cum_i)
        key_gain = jnp.exp(last - cum_i)
        key_end = (k.astype(F32) * key_gain).astype(BF16)
        query_start = (q.astype(F32) * query_gain).astype(BF16)
        gained_ref[at, 0:SPAN] = (g.astype(F32) * query_gain).astype(BF16)
        gained_ref[at, SPAN:2 * SPAN] = (v.astype(F32) * key_gain).astype(BF16)
        gained_ref[at, 2 * SPAN:] = key_end
        carried_ref[at, :] = dot(key_end, v, TN)
        pulled_ref[at, :] = dot(query_start, g, TN)
        weighted_ref[at, 0:SPAN] = (dot(g, v, NT) * weight).astype(BF16)
        weighted_ref[at, SPAN:2 * SPAN] = (dot(v, g, NT) * weight_t).astype(BF16)
        weighted_ref[at, 2 * SPAN:] = (dot(k, q, NT) * weight_t).astype(BF16)

    def second(b):
        base = b * SPAN
        at = pl.ds(pl.multiple_of(base, SPAN), SPAN)
        q, k, v, g = (chain_ref[at, a * SPAN:(a + 1) * SPAN] for a in range(4))
        state = low_ref[at, 0:SPAN]
        grad = low_ref[at, SPAN:]
        dq = dot(weighted_ref[at, 0:SPAN], k, NN) + dot(gained_ref[at, 0:SPAN], state, NT)
        dk = dot(weighted_ref[at, SPAN:2 * SPAN], q, NN) + dot(gained_ref[at, SPAN:2 * SPAN], grad, NT)
        dv = dot(weighted_ref[at, 2 * SPAN:], g, NN) + dot(gained_ref[at, 2 * SPAN:], grad, NN)
        term = jnp.sum(q.astype(F32) * dq - k.astype(F32) * dk, axis=1, keepdims=True)
        seg_i = segments(base + row_i, starts)
        seg_j = segments(base + iota((1, SPAN), 1), starts)
        lower = (seg_i == seg_j) & (row_i >= col_j)
        tail_ref[pl.ds(b, 1), :] = jnp.sum(jnp.where(lower, term, 0.0), axis=0, keepdims=True)
        key = key_ref[pl.ds(b, 1), 0:heads * window]
        hot = (key == (iota((SPAN, heads * window), 0) + 1).astype(F32)).astype(BF16)
        three = jnp.concatenate([dq.astype(BF16), dk.astype(BF16), dv.astype(BF16)], axis=1)
        back = dot(hot, three, TN).astype(BF16)
        for s in range(heads):
            begin = pl.multiple_of(at_ref[s, b], 16)
            for a in range(3):
                to = pl.ds(a * rows + begin, window)
                outs[s][to, :] += back[s * window:(s + 1) * window, a * SPAN:(a + 1) * SPAN]

    step = max(1, 64 // sources)

    @pl.loop(0, spans // step)
    def _(turn):
        for u in range(step):
            first(turn * step + u)

    def scan(turn, held):
        state, grad = held
        b, c = turn, spans - 1 - turn
        at_b = pl.ds(pl.multiple_of(b * SPAN, SPAN), SPAN)
        at_c = pl.ds(pl.multiple_of(c * SPAN, SPAN), SPAN)
        low_ref[at_b, 0:SPAN] = state.astype(BF16)
        low_ref[at_c, SPAN:] = grad.astype(BF16)
        fade_b = jnp.exp(cum_ref[pl.ds(b, 1), SPAN - 1:])
        fade_c = jnp.exp(cum_ref[pl.ds(c, 1), SPAN - 1:])
        return fade_b * state + carried_ref[at_b, :], fade_c * grad + pulled_ref[at_c, :]

    empty = jnp.zeros((SPAN, SPAN), F32)

    def scans(turn, held):
        for u in range(4):
            held = scan(turn * 4 + u, held)
        return held

    lax.fori_loop(0, spans // 4, scans, (empty, empty))

    @pl.loop(0, spans // step)
    def _(turn):
        for u in range(step):
            second(turn * step + u)

    firsts = jnp.transpose(tail_ref[...])[0:1, :]
    local = tail_ref[0:tall, :]
    seg_last = segments(iota((tall, SPAN), 0) * SPAN + SPAN - 1, starts)
    seg_first = segments(iota((tall, SPAN), 1) * SPAN, starts)
    later = (iota((tall, SPAN), 1) > iota((tall, SPAN), 0)) & (seg_first == seg_last)
    carry = jnp.sum(jnp.where(later, firsts, 0.0), axis=1, keepdims=True)
    full = local + jnp.where(segments(place, starts) == seg_last, carry, 0.0)
    begins = place == starts[0]
    for start in starts[1:]:
        begins = begins | (place == start)
    tails = jnp.where(begins, 0.0, full).astype(BF16)
    for s in range(heads):
        hot = (lo_ref[s:s + 1, :] == (iota((SPAN, rows), 0) + 1).astype(F32)).astype(BF16)
        found = dot(tails, hot, NN)
        mine = hi_ref[s:s + 1, :] == iota((tall, rows), 0).astype(F32)
        found = jnp.sum(jnp.where(mine, found, 0.0), axis=0, keepdims=True)
        outs[s][3 * rows:, :] = jnp.broadcast_to(found, (META, rows)).astype(BF16)


def unpack_kernel(chip_ref, pos_ref, *refs):
    heads = len(refs) - 4
    blocks, outs = refs[:heads], refs[heads:]
    rows = outs[0].shape[0]
    chip = chip_ref[0]
    _, rank = order(pos_ref[...])
    loose = (rank == iota((rows, rows), 1)).astype(BF16)
    line = iota((META, rows), 0)
    tails = jnp.zeros((META, rows), F32)
    for s in range(heads):
        head = chip ^ ((heads - s) % heads)
        at = pl.ds(pl.multiple_of(head * SPAN, SPAN), SPAN)
        together = jnp.concatenate([blocks[s][a * rows:(a + 1) * rows, :] for a in range(3)], axis=1)
        together = dot(loose, together, NN).astype(BF16)
        for a in range(3):
            outs[a][:, at] = together[:, a * SPAN:(a + 1) * SPAN]
        tails = jnp.where(line == head, blocks[s][3 * rows:, :].astype(F32), tails)
    outs[3][...] = dot(tails.astype(BF16), loose, NT)[:heads].astype(BF16)


def body(queries, keys, values, out_grad, log_decay, frame_pos, trial_lengths):
    rows, width = queries.shape
    heads = log_decay.shape[1]
    peers = lax.axis_size("ctx")
    cores = peers // heads
    frames = rows * peers
    spans = frames // SPAN
    chip = (lax.axis_index("ctx") // cores).astype(I32).reshape(1)

    def across(x, s):
        return lax.ppermute(x, "ctx", [(p, p ^ (s * cores)) for p in range(peers)])

    def beside(x, t):
        return lax.ppermute(x, "ctx", [(p, p ^ t) for p in range(peers)])

    packets = pl.pallas_call(
        pack_kernel,
        out_shape=[jax.ShapeDtypeStruct((4 * rows + META, SPAN), BF16)] * heads,
        in_specs=[SMEM] + [VMEM] * 6,
        out_specs=[VMEM] * heads,
        name="pack",
    )(chip, queries, keys, values, out_grad, log_decay.T, frame_pos.reshape(1, rows))
    got = [packets[0]] + [across(packets[s], heads - s) for s in range(1, heads)]
    everything = list(got)
    for t in range(1, cores):
        everything += [beside(x, t) for x in got]

    tall = max(META, spans)
    back = pl.pallas_call(
        functools.partial(chain_kernel, heads),
        out_shape=[jax.ShapeDtypeStruct((3 * rows + META, SPAN), BF16)] * heads,
        in_specs=[SMEM] + [VMEM] * peers,
        out_specs=[VMEM] * heads,
        scratch_shapes=[
            pltpu.VMEM((peers, SPAN), F32),
            pltpu.VMEM((peers, SPAN), F32),
            pltpu.VMEM((peers, SPAN), I32),
            pltpu.SMEM((peers, SPAN), I32),
            pltpu.SemaphoreType.DMA,
            pltpu.VMEM((spans, peers * (16 * pl.cdiv(2 * rows // peers, 16) + 16)), F32),
            pltpu.VMEM((tall, SPAN), F32),
            pltpu.VMEM((frames, 4 * SPAN), BF16),
            pltpu.VMEM((frames, 3 * SPAN), BF16),
            pltpu.VMEM((frames, 3 * SPAN), BF16),
            pltpu.VMEM((frames, SPAN), F32),
            pltpu.VMEM((frames, SPAN), F32),
            pltpu.VMEM((frames, 2 * SPAN), BF16),
            pltpu.VMEM((SPAN, SPAN), F32),
        ],
        compiler_params=pltpu.CompilerParams(vmem_limit_bytes=60 * 2**20),
        name="chain",
    )(trial_lengths, *everything)
    returned = [back[0]] + [across(back[s], heads - s) for s in range(1, heads)]

    *grads, tails = pl.pallas_call(
        unpack_kernel,
        out_shape=[jax.ShapeDtypeStruct((rows, width), BF16)] * 3 + [jax.ShapeDtypeStruct((heads, rows), BF16)],
        in_specs=[SMEM] + [VMEM] * (1 + heads),
        out_specs=[VMEM] * 4,
        name="unpack",
    )(chip, frame_pos.reshape(1, rows), *returned)
    return (*grads, tails.T)


def solution(mesh):
    rows = P(("groups", "ctx"), None)
    return jax.shard_map(
        body,
        mesh=mesh,
        in_specs=(rows, rows, rows, rows, rows, P(("groups", "ctx")), P("groups")),
        out_specs=(rows, rows, rows, rows),
        check_vma=False,
    )
```

```python
import functools

import jax
import jax.numpy as jnp
from jax import lax
from jax.experimental import pallas as pl
from jax.experimental.pallas import tpu as pltpu
from jax.sharding import PartitionSpec as P

SPAN = 128
META = 16
F32 = jnp.float32
BF16 = jnp.bfloat16
I32 = jnp.int32
VMEM = pl.BlockSpec(memory_space=pltpu.VMEM)
SMEM = pl.BlockSpec(memory_space=pltpu.SMEM)


def dot(a, b, dims):
    return lax.dot_general(a, b, ((dims[:1], dims[1:]), ((), ())), preferred_element_type=F32)


NN = (1, 0)
NT = (1, 1)
TN = (0, 0)


def iota(shape, dim):
    return lax.broadcasted_iota(I32, shape, dim)


def order(pos):
    rows = pos.shape[1]
    across = jnp.broadcast_to(pos.astype(F32), (rows, rows))
    down = jnp.transpose(across)
    as_row = jnp.sum((down < across).astype(F32), axis=0, keepdims=True)
    as_col = jnp.sum((across < down).astype(F32), axis=1, keepdims=True)
    return as_row.astype(I32), as_col.astype(I32)


def pack_kernel(chip_ref, *refs):
    given, outs, held, built, sems, leaves = refs[:6], refs[6:-9], refs[-9:-3], refs[-3], refs[-2], refs[-1]
    rows = given[0].shape[0]
    heads = len(outs)
    copies = [pltpu.make_async_copy(given[n], held[n], sems.at[n]) for n in range(6)]
    for n in (5, 4, 0, 1, 2, 3):
        copies[n].start()
    chip = chip_ref[0]
    copies[5].wait()
    pos = held[5][...]
    rank, _ = order(pos)
    sort = (rank == iota((rows, rows), 0)).astype(BF16)
    line = iota((META, rows), 0)
    where = jnp.where(line == 1, (pos // SPAN).astype(F32), jnp.where(line == 2, (pos % SPAN + 1).astype(F32), 0.0))
    where = dot(where.astype(BF16), sort, NT)
    copies[4].wait()
    decay = dot(held[4][...], sort, NT)
    for s in range(heads):
        head = chip ^ ((heads - s) % heads)
        mine = jnp.sum(jnp.where(iota((heads, rows), 0) == head, decay, 0.0), axis=0, keepdims=True)
        built[s, 4 * rows:, :] = jnp.where(line == 0, mine, where).astype(BF16)
    for a in range(4):
        copies[a].wait()
    for s in range(heads):
        head = chip ^ ((heads - s) % heads)
        at = pl.ds(pl.multiple_of(head * SPAN, SPAN), SPAN)
        together = jnp.concatenate([held[a][:, at] for a in range(4)], axis=1)
        together = dot(sort, together, NN).astype(BF16)
        for a in range(4):
            built[s, a * rows:(a + 1) * rows, :] = together[:, a * SPAN:(a + 1) * SPAN]
        pltpu.make_async_copy(built.at[s], outs[s], leaves.at[s]).start()
    for s in range(heads):
        pltpu.make_async_copy(built.at[s], outs[s], leaves.at[s]).wait()


def segments(position, starts):
    total = jnp.zeros_like(position)
    for start in starts:
        total = total + (position >= start).astype(I32)
    return total


def chain_kernel(heads, lengths_ref, *refs):
    sources = len(refs) - heads - 14
    blocks, outs, scratch = refs[:sources], refs[sources:sources + heads], refs[sources + heads:]
    (hi_ref, lo_ref, win_ref, at_ref, sem, down_ref, cum_ref, chain_ref, gained_ref, weighted_ref,
     carried_ref, pulled_ref, low_ref, tail_ref) = scratch
    rows = (blocks[0].shape[0] - META) // 4
    frames = rows * sources
    spans = frames // SPAN
    window = 16 * pl.cdiv(2 * rows // sources, 16) + 16
    tall = cum_ref.shape[0]
    starts = []
    total = jnp.int32(0)
    for t in range(lengths_ref.shape[0]):
        starts.append(total)
        total = total + lengths_ref[t]

    for n, ref in enumerate(blocks):
        meta = ref[4 * rows:, :].astype(F32)
        hi_ref[n:n + 1, :] = meta[1:2]
        lo_ref[n:n + 1, :] = meta[2:3]
    hi = hi_ref[...]
    lane = iota((sources, SPAN), 1)
    count = jnp.zeros((sources, SPAN), F32)
    for b in range(1, spans):
        ahead = jnp.sum((hi < b).astype(F32), axis=1, keepdims=True)
        count = jnp.where(lane == b, ahead, count)
    win_ref[...] = jnp.minimum((count.astype(I32) // 16) * 16, rows - window)
    copy = pltpu.make_async_copy(win_ref, at_ref, sem)
    copy.start()

    spread = []
    hots = []
    for n, ref in enumerate(blocks):
        meta = ref[4 * rows:, :].astype(F32)
        spread.append(jnp.where(meta[1:2] == iota((tall, rows), 0).astype(F32), meta[0:1], 0.0).astype(BF16))
        hots.append((meta[2:3] == (iota((SPAN, rows), 0) + 1).astype(F32)).astype(BF16))
    in_chain = dot(jnp.concatenate(spread, axis=1), jnp.concatenate(hots, axis=1), NT).astype(BF16)
    upper = (iota((SPAN, SPAN), 0) <= iota((SPAN, SPAN), 1)).astype(BF16)
    place = iota((tall, SPAN), 0) * SPAN + iota((tall, SPAN), 1)
    marks = segments(place, starts) - segments(iota((tall, SPAN), 0) * SPAN - 1, starts)
    cum_ref[...] = dot(in_chain, upper, NN) - 128.0 * marks.astype(F32)
    tail_ref[...] = jnp.zeros_like(tail_ref)
    for s, ref in enumerate(outs):
        ref[...] = jnp.zeros_like(ref)
        where = hi_ref[s:s + 1, :] * SPAN + lo_ref[s:s + 1, :] - 1.0
        down_ref[s * rows:(s + 1) * rows, :] = jnp.transpose(jnp.broadcast_to(where, (SPAN, rows)))

    row_i = iota((SPAN, SPAN), 0)
    col_j = iota((SPAN, SPAN), 1)
    per = SPAN // window
    copy.wait()

    def first(b):
        base = b * SPAN
        at = pl.ds(pl.multiple_of(base, SPAN), SPAN)
        keys = jnp.where(hi_ref[...] == b.astype(F32), lo_ref[...], 0.0)
        chain = jnp.zeros((SPAN, 4 * SPAN), F32)
        for n0 in range(0, sources, 2 * per):
            parts, found = [], []
            for n1 in range(n0, n0 + 2 * per, per):
                row = None
                for n in range(n1, n1 + per):
                    begin = pl.multiple_of(at_ref[n, b], 16)
                    turned = pltpu.roll(keys[n:n + 1], (n - n1) * window + SPAN - begin, 1)
                    row = turned if row is None else row + turned
                    found.append(jnp.concatenate(
                        [blocks[n][pl.ds(a * rows + begin, window), :] for a in range(4)], axis=1))
                parts.append(row)
            row = jnp.concatenate(parts, axis=1)
            hot = (row == (iota((SPAN, 2 * per * window), 0) + 1).astype(F32)).astype(BF16)
            chain = chain + dot(hot, jnp.concatenate(found, axis=0), NN)
        chain = chain.astype(BF16)
        chain_ref[at, :] = chain
        q, k, v, g = (chain[:, a * SPAN:(a + 1) * SPAN] for a in range(4))
        cum_j = cum_ref[pl.ds(b, 1), :]
        cum_i = jnp.transpose(jnp.broadcast_to(cum_j, (SPAN, SPAN)))
        last = cum_j[:, SPAN - 1:]
        gap = cum_i - cum_j
        weight = jnp.where(row_i >= col_j, jnp.exp(jnp.minimum(gap, 0.0)), 0.0)
        weight_t = jnp.where(row_i <= col_j, jnp.exp(jnp.minimum(-gap, 0.0)), 0.0)
        query_gain = jnp.exp(cum_i)
        key_gain = jnp.exp(last - cum_i)
        key_end = (k.astype(F32) * key_gain).astype(BF16)
        query_start = (q.astype(F32) * query_gain).astype(BF16)
        gained_ref[at, 0:SPAN] = (g.astype(F32) * query_gain).astype(BF16)
        gained_ref[at, SPAN:2 * SPAN] = (v.astype(F32) * key_gain).astype(BF16)
        gained_ref[at, 2 * SPAN:] = key_end
        carried_ref[at, :] = dot(key_end, v, TN)
        pulled_ref[at, :] = dot(query_start, g, TN)
        weighted_ref[at, 0:SPAN] = (dot(g, v, NT) * weight).astype(BF16)
        weighted_ref[at, SPAN:2 * SPAN] = (dot(v, g, NT) * weight_t).astype(BF16)
        weighted_ref[at, 2 * SPAN:] = (dot(k, q, NT) * weight_t).astype(BF16)

    def second(b):
        base = b * SPAN
        at = pl.ds(pl.multiple_of(base, SPAN), SPAN)
        q, k, v, g = (chain_ref[at, a * SPAN:(a + 1) * SPAN] for a in range(4))
        state = low_ref[at, 0:SPAN]
        grad = low_ref[at, SPAN:]
        dq = dot(weighted_ref[at, 0:SPAN], k, NN) + dot(gained_ref[at, 0:SPAN], state, NT)
        dk = dot(weighted_ref[at, SPAN:2 * SPAN], q, NN) + dot(gained_ref[at, SPAN:2 * SPAN], grad, NT)
        dv = dot(weighted_ref[at, 2 * SPAN:], g, NN) + dot(gained_ref[at, 2 * SPAN:], grad, NN)
        term = jnp.sum(q.astype(F32) * dq - k.astype(F32) * dk, axis=1, keepdims=True)
        seg_i = segments(base + row_i, starts)
        seg_j = segments(base + iota((1, SPAN), 1), starts)
        lower = (seg_i == seg_j) & (row_i >= col_j)
        tail_ref[pl.ds(b, 1), :] = jnp.sum(jnp.where(lower, term, 0.0), axis=0, keepdims=True)
        begins = [pl.multiple_of(at_ref[s, b], 16) for s in range(heads)]
        there = jnp.concatenate([down_ref[pl.ds(s * rows + begins[s], window), :] for s in range(heads)], axis=0)
        hot = (there == (base + iota((heads * window, SPAN), 1)).astype(F32)).astype(BF16)
        three = jnp.concatenate([dq.astype(BF16), dk.astype(BF16), dv.astype(BF16)], axis=1)
        back = dot(hot, three, NN).astype(BF16)
        for s in range(heads):
            for a in range(3):
                to = pl.ds(a * rows + begins[s], window)
                outs[s][to, :] += back[s * window:(s + 1) * window, a * SPAN:(a + 1) * SPAN]

    step = max(1, 128 // sources)

    @pl.loop(0, spans // step)
    def _(turn):
        for u in range(step):
            first(turn * step + u)

    def scan(turn, held):
        state, grad = held
        b, c = turn, spans - 1 - turn
        at_b = pl.ds(pl.multiple_of(b * SPAN, SPAN), SPAN)
        at_c = pl.ds(pl.multiple_of(c * SPAN, SPAN), SPAN)
        low_ref[at_b, 0:SPAN] = state.astype(BF16)
        low_ref[at_c, SPAN:] = grad.astype(BF16)
        fade_b = jnp.exp(cum_ref[pl.ds(b, 1), SPAN - 1:])
        fade_c = jnp.exp(cum_ref[pl.ds(c, 1), SPAN - 1:])
        return fade_b * state + carried_ref[at_b, :], fade_c * grad + pulled_ref[at_c, :]

    empty = jnp.zeros((SPAN, SPAN), F32)

    def scans(turn, held):
        for u in range(4):
            held = scan(turn * 4 + u, held)
        return held

    lax.fori_loop(0, spans // 4, scans, (empty, empty))

    @pl.loop(0, spans // step)
    def _(turn):
        for u in range(step):
            second(turn * step + u)

    firsts = jnp.transpose(tail_ref[...])[0:1, :]
    local = tail_ref[0:tall, :]
    seg_last = segments(iota((tall, SPAN), 0) * SPAN + SPAN - 1, starts)
    seg_first = segments(iota((tall, SPAN), 1) * SPAN, starts)
    later = (iota((tall, SPAN), 1) > iota((tall, SPAN), 0)) & (seg_first == seg_last)
    carry = jnp.sum(jnp.where(later, firsts, 0.0), axis=1, keepdims=True)
    full = local + jnp.where(segments(place, starts) == seg_last, carry, 0.0)
    begins = place == starts[0]
    for start in starts[1:]:
        begins = begins | (place == start)
    tails = jnp.where(begins, 0.0, full).astype(BF16)
    for s in range(heads):
        hot = (lo_ref[s:s + 1, :] == (iota((SPAN, rows), 0) + 1).astype(F32)).astype(BF16)
        found = dot(tails, hot, NN)
        mine = hi_ref[s:s + 1, :] == iota((tall, rows), 0).astype(F32)
        found = jnp.sum(jnp.where(mine, found, 0.0), axis=0, keepdims=True)
        outs[s][3 * rows:, :] = jnp.broadcast_to(found, (META, rows)).astype(BF16)


def unpack_kernel(chip_ref, pos_ref, *refs):
    heads = len(refs) - 4
    blocks, outs = refs[:heads], refs[heads:]
    rows = outs[0].shape[0]
    chip = chip_ref[0]
    _, rank = order(pos_ref[...])
    loose = (rank == iota((rows, rows), 1)).astype(BF16)
    line = iota((META, rows), 0)
    tails = jnp.zeros((META, rows), F32)
    for s in range(heads):
        head = chip ^ ((heads - s) % heads)
        at = pl.ds(pl.multiple_of(head * SPAN, SPAN), SPAN)
        together = jnp.concatenate([blocks[s][a * rows:(a + 1) * rows, :] for a in range(3)], axis=1)
        together = dot(loose, together, NN).astype(BF16)
        for a in range(3):
            outs[a][:, at] = together[:, a * SPAN:(a + 1) * SPAN]
        tails = jnp.where(line == head, blocks[s][3 * rows:, :].astype(F32), tails)
    outs[3][...] = dot(tails.astype(BF16), loose, NT)[:heads].astype(BF16)


def body(queries, keys, values, out_grad, log_decay, frame_pos, trial_lengths):
    rows, width = queries.shape
    heads = log_decay.shape[1]
    peers = lax.axis_size("ctx")
    cores = peers // heads
    frames = rows * peers
    spans = frames // SPAN
    chip = (lax.axis_index("ctx") // cores).astype(I32).reshape(1)

    def across(x, s):
        return lax.ppermute(x, "ctx", [(p, p ^ (s * cores)) for p in range(peers)])

    def beside(x, t):
        return lax.ppermute(x, "ctx", [(p, p ^ t) for p in range(peers)])

    packets = pl.pallas_call(
        pack_kernel,
        out_shape=[jax.ShapeDtypeStruct((4 * rows + META, SPAN), BF16)] * heads,
        in_specs=[SMEM] + [pl.BlockSpec(memory_space=pltpu.HBM)] * 6,
        out_specs=[pl.BlockSpec(memory_space=pltpu.HBM)] * heads,
        scratch_shapes=[pltpu.VMEM((rows, width), BF16)] * 4
        + [pltpu.VMEM((heads, rows), BF16), pltpu.VMEM((1, rows), I32), pltpu.VMEM((heads, 4 * rows + META, SPAN), BF16)]
        + [pltpu.SemaphoreType.DMA((6,)), pltpu.SemaphoreType.DMA((heads,))],
        compiler_params=pltpu.CompilerParams(vmem_limit_bytes=60 * 2**20),
        name="pack",
    )(chip, queries, keys, values, out_grad, log_decay.T, frame_pos.reshape(1, rows))
    got = [packets[0]] + [across(packets[s], heads - s) for s in range(1, heads)]
    everything = list(got)
    for t in range(1, cores):
        everything += [beside(x, t) for x in got]

    tall = max(META, spans)
    back = pl.pallas_call(
        functools.partial(chain_kernel, heads),
        out_shape=[jax.ShapeDtypeStruct((3 * rows + META, SPAN), BF16)] * heads,
        in_specs=[SMEM] + [VMEM] * peers,
        out_specs=[VMEM] * heads,
        scratch_shapes=[
            pltpu.VMEM((peers, SPAN), F32),
            pltpu.VMEM((peers, SPAN), F32),
            pltpu.VMEM((peers, SPAN), I32),
            pltpu.SMEM((peers, SPAN), I32),
            pltpu.SemaphoreType.DMA,
            pltpu.VMEM((heads * rows, SPAN), F32),
            pltpu.VMEM((tall, SPAN), F32),
            pltpu.VMEM((frames, 4 * SPAN), BF16),
            pltpu.VMEM((frames, 3 * SPAN), BF16),
            pltpu.VMEM((frames, 3 * SPAN), BF16),
            pltpu.VMEM((frames, SPAN), F32),
            pltpu.VMEM((frames, SPAN), F32),
            pltpu.VMEM((frames, 2 * SPAN), BF16),
            pltpu.VMEM((SPAN, SPAN), F32),
        ],
        compiler_params=pltpu.CompilerParams(vmem_limit_bytes=frames * 6 * 2**10 + 8 * 2**20),
        name="chain",
    )(trial_lengths, *everything)
    returned = [back[0]] + [across(back[s], heads - s) for s in range(1, heads)]

    *grads, tails = pl.pallas_call(
        unpack_kernel,
        out_shape=[jax.ShapeDtypeStruct((rows, width), BF16)] * 3 + [jax.ShapeDtypeStruct((heads, rows), BF16)],
        in_specs=[SMEM] + [VMEM] * (1 + heads),
        out_specs=[VMEM] * 4,
        compiler_params=pltpu.CompilerParams(vmem_limit_bytes=12 * 2**20),
        name="unpack",
    )(chip, frame_pos.reshape(1, rows), *returned)
    return (*grads, tails.T)


def solution(mesh):
    rows = P(("groups", "ctx"), None)
    return jax.shard_map(
        body,
        mesh=mesh,
        in_specs=(rows, rows, rows, rows, rows, P(("groups", "ctx")), P("groups")),
        out_specs=(rows, rows, rows, rows),
        check_vma=False,
    )
```

```python
import functools

import jax
import jax.numpy as jnp
from jax import lax
from jax.experimental import pallas as pl
from jax.experimental.pallas import tpu as pltpu
from jax.sharding import PartitionSpec as P

SPAN = 128
META = 16
COMING = (0, 1, 2, 6, 7, 4, 5, 3)
GOING = (0, 7, 6, 5, 4, 3, 2, 1)
TOGETHER = 3
F32 = jnp.float32
BF16 = jnp.bfloat16
I32 = jnp.int32
VMEM = pl.BlockSpec(memory_space=pltpu.VMEM)
SMEM = pl.BlockSpec(memory_space=pltpu.SMEM)


def dot(a, b, dims):
    return lax.dot_general(a, b, ((dims[:1], dims[1:]), ((), ())), preferred_element_type=F32)


NN = (1, 0)
NT = (1, 1)
TN = (0, 0)


def iota(shape, dim):
    return lax.broadcasted_iota(I32, shape, dim)


def order(pos):
    rows = pos.shape[1]
    across = jnp.broadcast_to(pos.astype(F32), (rows, rows))
    down = jnp.transpose(across)
    as_row = jnp.sum((down < across).astype(F32), axis=0, keepdims=True)
    as_col = jnp.sum((across < down).astype(F32), axis=1, keepdims=True)
    return as_row.astype(I32), as_col.astype(I32)


def pack_kernel(chip_ref, *refs):
    given, outs, held, built, sems, leaves = refs[:6], refs[6:-9], refs[-9:-3], refs[-3], refs[-2], refs[-1]
    rows = given[0].shape[0]
    heads = len(outs)
    copies = [pltpu.make_async_copy(given[n], held[n], sems.at[n]) for n in range(6)]
    for n in (5, 4, 0, 1, 2, 3):
        copies[n].start()
    chip = chip_ref[0]
    copies[5].wait()
    pos = held[5][...]
    rank, _ = order(pos)
    sort = (rank == iota((rows, rows), 0)).astype(BF16)
    line = iota((META, rows), 0)
    where = jnp.where(line == 1, (pos // SPAN).astype(F32), jnp.where(line == 2, (pos % SPAN + 1).astype(F32), 0.0))
    where = dot(where.astype(BF16), sort, NT)
    copies[4].wait()
    decay = dot(held[4][...], sort, NT)
    for s in range(heads):
        head = chip ^ COMING[s]
        mine = jnp.sum(jnp.where(iota((heads, rows), 0) == head, decay, 0.0), axis=0, keepdims=True)
        built[s, 4 * rows:, :] = jnp.where(line == 0, mine, where).astype(BF16)
    for a in range(4):
        copies[a].wait()
    for s in range(heads):
        head = chip ^ COMING[s]
        at = pl.ds(pl.multiple_of(head * SPAN, SPAN), SPAN)
        together = jnp.concatenate([held[a][:, at] for a in range(4)], axis=1)
        together = dot(sort, together, NN).astype(BF16)
        for a in range(4):
            built[s, a * rows:(a + 1) * rows, :] = together[:, a * SPAN:(a + 1) * SPAN]
        pltpu.make_async_copy(built.at[s], outs[s], leaves.at[s]).start()
    for s in range(heads):
        pltpu.make_async_copy(built.at[s], outs[s], leaves.at[s]).wait()


def segments(position, starts):
    total = jnp.zeros_like(position)
    for start in starts:
        total = total + (position >= start).astype(I32)
    return total


def chain_kernel(heads, lengths_ref, *refs):
    given, answers, scratch = refs[:-heads - 14], refs[-heads - 14:-14], refs[-14:]
    size = min(ref.shape[0] for ref in given)
    blocks = [ref.at[at:at + size] for ref in given for at in range(0, ref.shape[0], size)]
    outs = [answers[GOING.index(s)] for s in COMING]
    sources = len(blocks)
    (hi_ref, lo_ref, win_ref, at_ref, sem, down_ref, cum_ref, chain_ref, gained_ref, weighted_ref,
     carried_ref, pulled_ref, low_ref, tail_ref) = scratch
    rows = (size - META) // 4
    frames = rows * sources
    spans = frames // SPAN
    window = 16 * pl.cdiv(2 * rows // sources, 16) + 16
    tall = cum_ref.shape[0]
    starts = []
    total = jnp.int32(0)
    for t in range(lengths_ref.shape[0]):
        starts.append(total)
        total = total + lengths_ref[t]

    for n, ref in enumerate(blocks):
        meta = ref[4 * rows:, :].astype(F32)
        hi_ref[n:n + 1, :] = meta[1:2]
        lo_ref[n:n + 1, :] = meta[2:3]
    hi = hi_ref[...]
    lane = iota((sources, SPAN), 1)
    count = jnp.zeros((sources, SPAN), F32)
    for b in range(1, spans):
        ahead = jnp.sum((hi < b).astype(F32), axis=1, keepdims=True)
        count = jnp.where(lane == b, ahead, count)
    win_ref[...] = jnp.minimum((count.astype(I32) // 16) * 16, rows - window)
    copy = pltpu.make_async_copy(win_ref, at_ref, sem)
    copy.start()

    spread = []
    hots = []
    for n, ref in enumerate(blocks):
        meta = ref[4 * rows:, :].astype(F32)
        spread.append(jnp.where(meta[1:2] == iota((tall, rows), 0).astype(F32), meta[0:1], 0.0).astype(BF16))
        hots.append((meta[2:3] == (iota((SPAN, rows), 0) + 1).astype(F32)).astype(BF16))
    in_chain = dot(jnp.concatenate(spread, axis=1), jnp.concatenate(hots, axis=1), NT).astype(BF16)
    upper = (iota((SPAN, SPAN), 0) <= iota((SPAN, SPAN), 1)).astype(BF16)
    place = iota((tall, SPAN), 0) * SPAN + iota((tall, SPAN), 1)
    marks = segments(place, starts) - segments(iota((tall, SPAN), 0) * SPAN - 1, starts)
    cum_ref[...] = dot(in_chain, upper, NN) - 128.0 * marks.astype(F32)
    tail_ref[...] = jnp.zeros_like(tail_ref)
    for s, ref in enumerate(outs):
        ref[...] = jnp.zeros_like(ref)
        where = hi_ref[s:s + 1, :] * SPAN + lo_ref[s:s + 1, :] - 1.0
        down_ref[s * rows:(s + 1) * rows, :] = jnp.transpose(jnp.broadcast_to(where, (SPAN, rows)))

    row_i = iota((SPAN, SPAN), 0)
    col_j = iota((SPAN, SPAN), 1)
    per = SPAN // window
    copy.wait()

    def first(b):
        base = b * SPAN
        at = pl.ds(pl.multiple_of(base, SPAN), SPAN)
        keys = jnp.where(hi_ref[...] == b.astype(F32), lo_ref[...], 0.0)
        chain = jnp.zeros((SPAN, 4 * SPAN), F32)
        for n0 in range(0, sources, 2 * per):
            parts, found = [], []
            for n1 in range(n0, n0 + 2 * per, per):
                row = None
                for n in range(n1, n1 + per):
                    begin = pl.multiple_of(at_ref[n, b], 16)
                    turned = pltpu.roll(keys[n:n + 1], (n - n1) * window + SPAN - begin, 1)
                    row = turned if row is None else row + turned
                    found.append(jnp.concatenate(
                        [blocks[n][pl.ds(a * rows + begin, window), :] for a in range(4)], axis=1))
                parts.append(row)
            row = jnp.concatenate(parts, axis=1)
            hot = (row == (iota((SPAN, 2 * per * window), 0) + 1).astype(F32)).astype(BF16)
            chain = chain + dot(hot, jnp.concatenate(found, axis=0), NN)
        chain = chain.astype(BF16)
        chain_ref[at, :] = chain
        q, k, v, g = (chain[:, a * SPAN:(a + 1) * SPAN] for a in range(4))
        cum_j = cum_ref[pl.ds(b, 1), :]
        cum_i = jnp.transpose(jnp.broadcast_to(cum_j, (SPAN, SPAN)))
        last = cum_j[:, SPAN - 1:]
        gap = cum_i - cum_j
        weight = jnp.where(row_i >= col_j, jnp.exp(jnp.minimum(gap, 0.0)), 0.0)
        weight_t = jnp.where(row_i <= col_j, jnp.exp(jnp.minimum(-gap, 0.0)), 0.0)
        query_gain = jnp.exp(cum_i)
        key_gain = jnp.exp(last - cum_i)
        key_end = (k.astype(F32) * key_gain).astype(BF16)
        query_start = (q.astype(F32) * query_gain).astype(BF16)
        gained_ref[at, 0:SPAN] = (g.astype(F32) * query_gain).astype(BF16)
        gained_ref[at, SPAN:2 * SPAN] = (v.astype(F32) * key_gain).astype(BF16)
        gained_ref[at, 2 * SPAN:] = key_end
        carried_ref[at, :] = dot(key_end, v, TN)
        pulled_ref[at, :] = dot(query_start, g, TN)
        weighted_ref[at, 0:SPAN] = (dot(g, v, NT) * weight).astype(BF16)
        weighted_ref[at, SPAN:2 * SPAN] = (dot(v, g, NT) * weight_t).astype(BF16)
        weighted_ref[at, 2 * SPAN:] = (dot(k, q, NT) * weight_t).astype(BF16)

    def second(b):
        base = b * SPAN
        at = pl.ds(pl.multiple_of(base, SPAN), SPAN)
        q, k, v, g = (chain_ref[at, a * SPAN:(a + 1) * SPAN] for a in range(4))
        state = low_ref[at, 0:SPAN]
        grad = low_ref[at, SPAN:]
        dq = dot(weighted_ref[at, 0:SPAN], k, NN) + dot(gained_ref[at, 0:SPAN], state, NT)
        dk = dot(weighted_ref[at, SPAN:2 * SPAN], q, NN) + dot(gained_ref[at, SPAN:2 * SPAN], grad, NT)
        dv = dot(weighted_ref[at, 2 * SPAN:], g, NN) + dot(gained_ref[at, 2 * SPAN:], grad, NN)
        term = jnp.sum(q.astype(F32) * dq - k.astype(F32) * dk, axis=1, keepdims=True)
        seg_i = segments(base + row_i, starts)
        seg_j = segments(base + iota((1, SPAN), 1), starts)
        lower = (seg_i == seg_j) & (row_i >= col_j)
        tail_ref[pl.ds(b, 1), :] = jnp.sum(jnp.where(lower, term, 0.0), axis=0, keepdims=True)
        begins = [pl.multiple_of(at_ref[s, b], 16) for s in range(heads)]
        there = jnp.concatenate([down_ref[pl.ds(s * rows + begins[s], window), :] for s in range(heads)], axis=0)
        hot = (there == (base + iota((heads * window, SPAN), 1)).astype(F32)).astype(BF16)
        three = jnp.concatenate([dq.astype(BF16), dk.astype(BF16), dv.astype(BF16)], axis=1)
        back = dot(hot, three, NN).astype(BF16)
        for s in range(heads):
            for a in range(3):
                to = pl.ds(a * rows + begins[s], window)
                outs[s][to, :] += back[s * window:(s + 1) * window, a * SPAN:(a + 1) * SPAN]

    step = max(1, 128 // sources)

    @pl.loop(0, spans // step)
    def _(turn):
        for u in range(step):
            first(turn * step + u)

    def scan(turn, held):
        state, grad = held
        b, c = turn, spans - 1 - turn
        at_b = pl.ds(pl.multiple_of(b * SPAN, SPAN), SPAN)
        at_c = pl.ds(pl.multiple_of(c * SPAN, SPAN), SPAN)
        low_ref[at_b, 0:SPAN] = state.astype(BF16)
        low_ref[at_c, SPAN:] = grad.astype(BF16)
        fade_b = jnp.exp(cum_ref[pl.ds(b, 1), SPAN - 1:])
        fade_c = jnp.exp(cum_ref[pl.ds(c, 1), SPAN - 1:])
        return fade_b * state + carried_ref[at_b, :], fade_c * grad + pulled_ref[at_c, :]

    empty = jnp.zeros((SPAN, SPAN), F32)

    def scans(turn, held):
        for u in range(4):
            held = scan(turn * 4 + u, held)
        return held

    lax.fori_loop(0, spans // 4, scans, (empty, empty))

    @pl.loop(0, spans // step)
    def _(turn):
        for u in range(step):
            second(turn * step + u)

    firsts = jnp.transpose(tail_ref[...])[0:1, :]
    local = tail_ref[0:tall, :]
    seg_last = segments(iota((tall, SPAN), 0) * SPAN + SPAN - 1, starts)
    seg_first = segments(iota((tall, SPAN), 1) * SPAN, starts)
    later = (iota((tall, SPAN), 1) > iota((tall, SPAN), 0)) & (seg_first == seg_last)
    carry = jnp.sum(jnp.where(later, firsts, 0.0), axis=1, keepdims=True)
    full = local + jnp.where(segments(place, starts) == seg_last, carry, 0.0)
    begins = place == starts[0]
    for start in starts[1:]:
        begins = begins | (place == start)
    tails = jnp.where(begins, 0.0, full).astype(BF16)
    for s in range(heads):
        hot = (lo_ref[s:s + 1, :] == (iota((SPAN, rows), 0) + 1).astype(F32)).astype(BF16)
        found = dot(tails, hot, NN)
        mine = hi_ref[s:s + 1, :] == iota((tall, rows), 0).astype(F32)
        found = jnp.sum(jnp.where(mine, found, 0.0), axis=0, keepdims=True)
        outs[s][3 * rows:, :] = jnp.broadcast_to(found, (META, rows)).astype(BF16)


def join_kernel(*refs):
    size = refs[0].shape[0]
    for n, ref in enumerate(refs[:-1]):
        refs[-1][n * size:(n + 1) * size, :] = ref[...]


def unpack_kernel(chip_ref, pos_ref, *refs):
    heads = len(refs) - 4
    blocks, outs = refs[:heads], refs[heads:]
    rows = outs[0].shape[0]
    chip = chip_ref[0]
    _, rank = order(pos_ref[...])
    loose = (rank == iota((rows, rows), 1)).astype(BF16)
    line = iota((META, rows), 0)
    tails = jnp.zeros((META, rows), F32)
    for s in range(heads):
        head = chip ^ GOING[s]
        at = pl.ds(pl.multiple_of(head * SPAN, SPAN), SPAN)
        together = jnp.concatenate([blocks[s][a * rows:(a + 1) * rows, :] for a in range(3)], axis=1)
        together = dot(loose, together, NN).astype(BF16)
        for a in range(3):
            outs[a][:, at] = together[:, a * SPAN:(a + 1) * SPAN]
        tails = jnp.where(line == head, blocks[s][3 * rows:, :].astype(F32), tails)
    outs[3][...] = dot(tails.astype(BF16), loose, NT)[:heads].astype(BF16)


def body(queries, keys, values, out_grad, log_decay, frame_pos, trial_lengths):
    rows, width = queries.shape
    heads = log_decay.shape[1]
    peers = lax.axis_size("ctx")
    cores = peers // heads
    frames = rows * peers
    spans = frames // SPAN
    chip = (lax.axis_index("ctx") // cores).astype(I32).reshape(1)

    def across(x, s):
        return lax.ppermute(x, "ctx", [(p, p ^ (s * cores)) for p in range(peers)])

    def beside(x, t):
        return lax.ppermute(x, "ctx", [(p, p ^ t) for p in range(peers)])

    packets = pl.pallas_call(
        pack_kernel,
        out_shape=[jax.ShapeDtypeStruct((4 * rows + META, SPAN), BF16)] * heads,
        in_specs=[SMEM] + [pl.BlockSpec(memory_space=pltpu.HBM)] * 6,
        out_specs=[pl.BlockSpec(memory_space=pltpu.HBM)] * heads,
        scratch_shapes=[pltpu.VMEM((rows, width), BF16)] * 4
        + [pltpu.VMEM((heads, rows), BF16), pltpu.VMEM((1, rows), I32), pltpu.VMEM((heads, 4 * rows + META, SPAN), BF16)]
        + [pltpu.SemaphoreType.DMA((6,)), pltpu.SemaphoreType.DMA((heads,))],
        compiler_params=pltpu.CompilerParams(vmem_limit_bytes=60 * 2**20),
        name="pack",
    )(chip, queries, keys, values, out_grad, log_decay.T, frame_pos.reshape(1, rows))
    got = [packets[0]] + [across(packets[s], COMING[s]) for s in range(1, heads)]
    size = 4 * rows + META
    joined = pl.pallas_call(
        join_kernel,
        out_shape=jax.ShapeDtypeStruct((TOGETHER * size, SPAN), BF16),
        in_specs=[VMEM] * TOGETHER,
        out_specs=VMEM,
        compiler_params=pltpu.CompilerParams(vmem_limit_bytes=4 * 2**20),
        cost_estimate=pl.CostEstimate(flops=2**30, bytes_accessed=2**18, transcendentals=0),
        name="join",
    )(*got[:TOGETHER])
    got = [joined, *got[TOGETHER:]]
    everything = list(got)
    for t in range(1, cores):
        everything += [beside(x, t) for x in got]

    tall = max(META, spans)
    back = pl.pallas_call(
        functools.partial(chain_kernel, heads),
        out_shape=[jax.ShapeDtypeStruct((3 * rows + META, SPAN), BF16)] * heads,
        in_specs=[SMEM] + [VMEM] * len(everything),
        out_specs=[VMEM] * heads,
        scratch_shapes=[
            pltpu.VMEM((peers, SPAN), F32),
            pltpu.VMEM((peers, SPAN), F32),
            pltpu.VMEM((peers, SPAN), I32),
            pltpu.SMEM((peers, SPAN), I32),
            pltpu.SemaphoreType.DMA,
            pltpu.VMEM((heads * rows, SPAN), F32),
            pltpu.VMEM((tall, SPAN), F32),
            pltpu.VMEM((frames, 4 * SPAN), BF16),
            pltpu.VMEM((frames, 3 * SPAN), BF16),
            pltpu.VMEM((frames, 3 * SPAN), BF16),
            pltpu.VMEM((frames, SPAN), F32),
            pltpu.VMEM((frames, SPAN), F32),
            pltpu.VMEM((frames, 2 * SPAN), BF16),
            pltpu.VMEM((SPAN, SPAN), F32),
        ],
        compiler_params=pltpu.CompilerParams(vmem_limit_bytes=frames * 6 * 2**10 + 8 * 2**20),
        name="chain",
    )(trial_lengths, *everything)
    returned = [back[0]] + [across(back[s], GOING[s]) for s in range(1, heads)]

    *grads, tails = pl.pallas_call(
        unpack_kernel,
        out_shape=[jax.ShapeDtypeStruct((rows, width), BF16)] * 3 + [jax.ShapeDtypeStruct((heads, rows), BF16)],
        in_specs=[SMEM] + [VMEM] * (1 + heads),
        out_specs=[VMEM] * 4,
        compiler_params=pltpu.CompilerParams(vmem_limit_bytes=12 * 2**20),
        name="unpack",
    )(chip, frame_pos.reshape(1, rows), *returned)
    return (*grads, tails.T)


def solution(mesh):
    rows = P(("groups", "ctx"), None)
    return jax.shard_map(
        body,
        mesh=mesh,
        in_specs=(rows, rows, rows, rows, rows, P(("groups", "ctx")), P("groups")),
        out_specs=(rows, rows, rows, rows),
        check_vma=False,
    )
```

```python
import functools

import jax
import jax.numpy as jnp
from jax import lax
from jax.experimental import pallas as pl
from jax.experimental.pallas import tpu as pltpu
from jax.sharding import PartitionSpec as P

SPAN = 128
META = 16
COMING = (0, 1, 2, 6, 7, 4, 5, 3)
GOING = (0, 7, 6, 5, 4, 3, 2, 1)
TOGETHER = 3
F32 = jnp.float32
BF16 = jnp.bfloat16
I32 = jnp.int32
VMEM = pl.BlockSpec(memory_space=pltpu.VMEM)
SMEM = pl.BlockSpec(memory_space=pltpu.SMEM)


def dot(a, b, dims):
    return lax.dot_general(a, b, ((dims[:1], dims[1:]), ((), ())), preferred_element_type=F32)


NN = (1, 0)
NT = (1, 1)
TN = (0, 0)


def iota(shape, dim):
    return lax.broadcasted_iota(I32, shape, dim)


def order(pos):
    rows = pos.shape[1]
    across = jnp.broadcast_to(pos.astype(F32), (rows, rows))
    down = jnp.transpose(across)
    as_row = jnp.sum((down < across).astype(F32), axis=0, keepdims=True)
    as_col = jnp.sum((across < down).astype(F32), axis=1, keepdims=True)
    return as_row.astype(I32), as_col.astype(I32)


def pack_kernel(chip_ref, *refs):
    given, outs, held, built, sems, leaves = refs[:6], refs[6:-9], refs[-9:-3], refs[-3], refs[-2], refs[-1]
    rows = given[0].shape[0]
    heads = len(outs)
    copies = [pltpu.make_async_copy(given[n], held[n], sems.at[n]) for n in range(6)]
    for n in (5, 4, 0, 1, 2, 3):
        copies[n].start()
    chip = chip_ref[0]
    copies[5].wait()
    pos = held[5][...]
    rank, _ = order(pos)
    sort = (rank == iota((rows, rows), 0)).astype(BF16)
    line = iota((META, rows), 0)
    where = jnp.where(line == 1, (pos // SPAN).astype(F32), jnp.where(line == 2, (pos % SPAN + 1).astype(F32), 0.0))
    where = dot(where.astype(BF16), sort, NT)
    copies[4].wait()
    decay = dot(held[4][...], sort, NT)
    for s in range(heads):
        head = chip ^ COMING[s]
        mine = jnp.sum(jnp.where(iota((heads, rows), 0) == head, decay, 0.0), axis=0, keepdims=True)
        built[s, 4 * rows:, :] = jnp.where(line == 0, mine, where).astype(BF16)
    for a in range(4):
        copies[a].wait()
    for s in range(heads):
        head = chip ^ COMING[s]
        at = pl.ds(pl.multiple_of(head * SPAN, SPAN), SPAN)
        together = jnp.concatenate([held[a][:, at] for a in range(4)], axis=1)
        together = dot(sort, together, NN).astype(BF16)
        for a in range(4):
            built[s, a * rows:(a + 1) * rows, :] = together[:, a * SPAN:(a + 1) * SPAN]
        pltpu.make_async_copy(built.at[s], outs[s], leaves.at[s]).start()
    for s in range(heads):
        pltpu.make_async_copy(built.at[s], outs[s], leaves.at[s]).wait()


def segments(position, starts):
    total = jnp.zeros_like(position)
    for start in starts:
        total = total + (position >= start).astype(I32)
    return total


def chain_kernel(heads, lengths_ref, *refs):
    given, answers, scratch = refs[:-heads - 13], refs[-heads - 13:-13], refs[-13:]
    size = min(ref.shape[0] for ref in given)
    blocks = [ref.at[at:at + size] for ref in given for at in range(0, ref.shape[0], size)]
    outs = [answers[GOING.index(s)] for s in COMING]
    sources = len(blocks)
    (hi_ref, lo_ref, win_ref, at_ref, sem, down_ref, cum_ref, chain_ref, gained_ref, weighted_ref,
     pulled_ref, state_ref, tail_ref) = scratch
    rows = (size - META) // 4
    frames = rows * sources
    spans = frames // SPAN
    window = 16 * pl.cdiv(2 * rows // sources, 16) + 16
    tall = cum_ref.shape[0]
    starts = []
    total = jnp.int32(0)
    for t in range(lengths_ref.shape[0]):
        starts.append(total)
        total = total + lengths_ref[t]

    for n, ref in enumerate(blocks):
        meta = ref[4 * rows:, :].astype(F32)
        hi_ref[n:n + 1, :] = meta[1:2]
        lo_ref[n:n + 1, :] = meta[2:3]
    hi = hi_ref[...]
    lane = iota((sources, SPAN), 1)
    count = jnp.zeros((sources, SPAN), F32)
    for b in range(1, spans):
        ahead = jnp.sum((hi < b).astype(F32), axis=1, keepdims=True)
        count = jnp.where(lane == b, ahead, count)
    win_ref[...] = jnp.minimum((count.astype(I32) // 16) * 16, rows - window)
    copy = pltpu.make_async_copy(win_ref, at_ref, sem)
    copy.start()

    spread = []
    hots = []
    for n, ref in enumerate(blocks):
        meta = ref[4 * rows:, :].astype(F32)
        spread.append(jnp.where(meta[1:2] == iota((tall, rows), 0).astype(F32), meta[0:1], 0.0).astype(BF16))
        hots.append((meta[2:3] == (iota((SPAN, rows), 0) + 1).astype(F32)).astype(BF16))
    in_chain = dot(jnp.concatenate(spread, axis=1), jnp.concatenate(hots, axis=1), NT).astype(BF16)
    upper = (iota((SPAN, SPAN), 0) <= iota((SPAN, SPAN), 1)).astype(BF16)
    place = iota((tall, SPAN), 0) * SPAN + iota((tall, SPAN), 1)
    marks = segments(place, starts) - segments(iota((tall, SPAN), 0) * SPAN - 1, starts)
    cum_ref[...] = dot(in_chain, upper, NN) - 128.0 * marks.astype(F32)
    tail_ref[...] = jnp.zeros_like(tail_ref)
    for s, ref in enumerate(outs):
        ref[...] = jnp.zeros_like(ref)
        where = hi_ref[s:s + 1, :] * SPAN + lo_ref[s:s + 1, :] - 1.0
        down_ref[s * rows:(s + 1) * rows, :] = jnp.transpose(jnp.broadcast_to(where, (SPAN, rows)))

    row_i = iota((SPAN, SPAN), 0)
    col_j = iota((SPAN, SPAN), 1)
    per = SPAN // window
    copy.wait()

    def fade(b):
        return jnp.exp(cum_ref[pl.ds(b, 1), SPAN - 1:])

    def first(b, state):
        base = b * SPAN
        at = pl.ds(pl.multiple_of(base, SPAN), SPAN)
        keys = jnp.where(hi_ref[...] == b.astype(F32), lo_ref[...], 0.0)
        chain = jnp.zeros((SPAN, 4 * SPAN), F32)
        for n0 in range(0, sources, 2 * per):
            parts, found = [], []
            for n1 in range(n0, n0 + 2 * per, per):
                row = None
                for n in range(n1, n1 + per):
                    begin = pl.multiple_of(at_ref[n, b], 16)
                    turned = pltpu.roll(keys[n:n + 1], (n - n1) * window + SPAN - begin, 1)
                    row = turned if row is None else row + turned
                    found.append(jnp.concatenate(
                        [blocks[n][pl.ds(a * rows + begin, window), :] for a in range(4)], axis=1))
                parts.append(row)
            row = jnp.concatenate(parts, axis=1)
            hot = (row == (iota((SPAN, 2 * per * window), 0) + 1).astype(F32)).astype(BF16)
            chain = chain + dot(hot, jnp.concatenate(found, axis=0), NN)
        chain = chain.astype(BF16)
        chain_ref[at, :] = chain
        q, k, v, g = (chain[:, a * SPAN:(a + 1) * SPAN] for a in range(4))
        cum_j = cum_ref[pl.ds(b, 1), :]
        cum_i = jnp.transpose(jnp.broadcast_to(cum_j, (SPAN, SPAN)))
        last = cum_j[:, SPAN - 1:]
        gap = cum_i - cum_j
        weight = jnp.where(row_i >= col_j, jnp.exp(jnp.minimum(gap, 0.0)), 0.0)
        weight_t = jnp.where(row_i <= col_j, jnp.exp(jnp.minimum(-gap, 0.0)), 0.0)
        query_gain = jnp.exp(cum_i)
        key_gain = jnp.exp(last - cum_i)
        key_end = (k.astype(F32) * key_gain).astype(BF16)
        query_start = (q.astype(F32) * query_gain).astype(BF16)
        gained_ref[at, 0:SPAN] = (g.astype(F32) * query_gain).astype(BF16)
        gained_ref[at, SPAN:2 * SPAN] = (v.astype(F32) * key_gain).astype(BF16)
        gained_ref[at, 2 * SPAN:] = key_end
        state_ref[at, :] = state.astype(BF16)
        state = fade(b) * state + dot(key_end, v, TN)
        pulled_ref[at, :] = dot(query_start, g, TN)
        weighted_ref[at, 0:SPAN] = (dot(g, v, NT) * weight).astype(BF16)
        weighted_ref[at, SPAN:2 * SPAN] = (dot(v, g, NT) * weight_t).astype(BF16)
        weighted_ref[at, 2 * SPAN:] = (dot(k, q, NT) * weight_t).astype(BF16)
        return state

    def second(b, held):
        base = b * SPAN
        at = pl.ds(pl.multiple_of(base, SPAN), SPAN)
        q, k, v, g = (chain_ref[at, a * SPAN:(a + 1) * SPAN] for a in range(4))
        state = state_ref[at, :]
        grad = held.astype(BF16)
        dq = dot(weighted_ref[at, 0:SPAN], k, NN) + dot(gained_ref[at, 0:SPAN], state, NT)
        dk = dot(weighted_ref[at, SPAN:2 * SPAN], q, NN) + dot(gained_ref[at, SPAN:2 * SPAN], grad, NT)
        dv = dot(weighted_ref[at, 2 * SPAN:], g, NN) + dot(gained_ref[at, 2 * SPAN:], grad, NN)
        term = jnp.sum(q.astype(F32) * dq - k.astype(F32) * dk, axis=1, keepdims=True)
        seg_i = segments(base + row_i, starts)
        seg_j = segments(base + iota((1, SPAN), 1), starts)
        lower = (seg_i == seg_j) & (row_i >= col_j)
        tail_ref[pl.ds(b, 1), :] = jnp.sum(jnp.where(lower, term, 0.0), axis=0, keepdims=True)
        begins = [pl.multiple_of(at_ref[s, b], 16) for s in range(heads)]
        there = jnp.concatenate([down_ref[pl.ds(s * rows + begins[s], window), :] for s in range(heads)], axis=0)
        hot = (there == (base + iota((heads * window, SPAN), 1)).astype(F32)).astype(BF16)
        three = jnp.concatenate([dq.astype(BF16), dk.astype(BF16), dv.astype(BF16)], axis=1)
        back = dot(hot, three, NN).astype(BF16)
        for s in range(heads):
            for a in range(3):
                to = pl.ds(a * rows + begins[s], window)
                outs[s][to, :] += back[s * window:(s + 1) * window, a * SPAN:(a + 1) * SPAN]

        return fade(b) * held + pulled_ref[at, :]

    step = max(1, 128 // sources)
    empty = jnp.zeros((SPAN, SPAN), F32)

    def forward(turn, state):
        for u in range(step):
            state = first(turn * step + u, state)
        return state

    def backward(turn, grad):
        for u in range(step):
            grad = second(spans - 1 - turn * step - u, grad)
        return grad

    lax.fori_loop(0, spans // step, forward, empty)
    lax.fori_loop(0, spans // step, backward, empty)

    firsts = jnp.transpose(tail_ref[...])[0:1, :]
    local = tail_ref[0:tall, :]
    seg_last = segments(iota((tall, SPAN), 0) * SPAN + SPAN - 1, starts)
    seg_first = segments(iota((tall, SPAN), 1) * SPAN, starts)
    later = (iota((tall, SPAN), 1) > iota((tall, SPAN), 0)) & (seg_first == seg_last)
    carry = jnp.sum(jnp.where(later, firsts, 0.0), axis=1, keepdims=True)
    full = local + jnp.where(segments(place, starts) == seg_last, carry, 0.0)
    begins = place == starts[0]
    for start in starts[1:]:
        begins = begins | (place == start)
    tails = jnp.where(begins, 0.0, full).astype(BF16)
    for s in range(heads):
        hot = (lo_ref[s:s + 1, :] == (iota((SPAN, rows), 0) + 1).astype(F32)).astype(BF16)
        found = dot(tails, hot, NN)
        mine = hi_ref[s:s + 1, :] == iota((tall, rows), 0).astype(F32)
        found = jnp.sum(jnp.where(mine, found, 0.0), axis=0, keepdims=True)
        outs[s][3 * rows:, :] = jnp.broadcast_to(found, (META, rows)).astype(BF16)


def join_kernel(*refs):
    size = refs[0].shape[0]
    for n, ref in enumerate(refs[:-1]):
        refs[-1][n * size:(n + 1) * size, :] = ref[...]


def unpack_kernel(chip_ref, pos_ref, *refs):
    heads = len(refs) - 4
    blocks, outs = refs[:heads], refs[heads:]
    rows = outs[0].shape[0]
    chip = chip_ref[0]
    _, rank = order(pos_ref[...])
    loose = (rank == iota((rows, rows), 1)).astype(BF16)
    line = iota((META, rows), 0)
    tails = jnp.zeros((META, rows), F32)
    for s in range(heads):
        head = chip ^ GOING[s]
        at = pl.ds(pl.multiple_of(head * SPAN, SPAN), SPAN)
        together = jnp.concatenate([blocks[s][a * rows:(a + 1) * rows, :] for a in range(3)], axis=1)
        together = dot(loose, together, NN).astype(BF16)
        for a in range(3):
            outs[a][:, at] = together[:, a * SPAN:(a + 1) * SPAN]
        tails = jnp.where(line == head, blocks[s][3 * rows:, :].astype(F32), tails)
    outs[3][...] = dot(tails.astype(BF16), loose, NT)[:heads].astype(BF16)


def body(queries, keys, values, out_grad, log_decay, frame_pos, trial_lengths):
    rows, width = queries.shape
    heads = log_decay.shape[1]
    peers = lax.axis_size("ctx")
    cores = peers // heads
    frames = rows * peers
    spans = frames // SPAN
    chip = (lax.axis_index("ctx") // cores).astype(I32).reshape(1)

    def across(x, s):
        return lax.ppermute(x, "ctx", [(p, p ^ (s * cores)) for p in range(peers)])

    def beside(x, t):
        return lax.ppermute(x, "ctx", [(p, p ^ t) for p in range(peers)])

    packets = pl.pallas_call(
        pack_kernel,
        out_shape=[jax.ShapeDtypeStruct((4 * rows + META, SPAN), BF16)] * heads,
        in_specs=[SMEM] + [pl.BlockSpec(memory_space=pltpu.HBM)] * 6,
        out_specs=[pl.BlockSpec(memory_space=pltpu.HBM)] * heads,
        scratch_shapes=[pltpu.VMEM((rows, width), BF16)] * 4
        + [pltpu.VMEM((heads, rows), BF16), pltpu.VMEM((1, rows), I32), pltpu.VMEM((heads, 4 * rows + META, SPAN), BF16)]
        + [pltpu.SemaphoreType.DMA((6,)), pltpu.SemaphoreType.DMA((heads,))],
        compiler_params=pltpu.CompilerParams(vmem_limit_bytes=60 * 2**20),
        name="pack",
    )(chip, queries, keys, values, out_grad, log_decay.T, frame_pos.reshape(1, rows))
    got = [packets[0]] + [across(packets[s], COMING[s]) for s in range(1, heads)]
    size = 4 * rows + META
    joined = pl.pallas_call(
        join_kernel,
        out_shape=jax.ShapeDtypeStruct((TOGETHER * size, SPAN), BF16),
        in_specs=[VMEM] * TOGETHER,
        out_specs=VMEM,
        compiler_params=pltpu.CompilerParams(vmem_limit_bytes=4 * 2**20),
        cost_estimate=pl.CostEstimate(flops=2**30, bytes_accessed=2**18, transcendentals=0),
        name="join",
    )(*got[:TOGETHER])
    got = [joined, *got[TOGETHER:]]
    everything = list(got)
    for t in range(1, cores):
        everything += [beside(x, t) for x in got]

    tall = max(META, spans)
    back = pl.pallas_call(
        functools.partial(chain_kernel, heads),
        out_shape=[jax.ShapeDtypeStruct((3 * rows + META, SPAN), BF16)] * heads,
        in_specs=[SMEM] + [VMEM] * len(everything),
        out_specs=[VMEM] * heads,
        scratch_shapes=[
            pltpu.VMEM((peers, SPAN), F32),
            pltpu.VMEM((peers, SPAN), F32),
            pltpu.VMEM((peers, SPAN), I32),
            pltpu.SMEM((peers, SPAN), I32),
            pltpu.SemaphoreType.DMA,
            pltpu.VMEM((heads * rows, SPAN), F32),
            pltpu.VMEM((tall, SPAN), F32),
            pltpu.VMEM((frames, 4 * SPAN), BF16),
            pltpu.VMEM((frames, 3 * SPAN), BF16),
            pltpu.VMEM((frames, 3 * SPAN), BF16),
            pltpu.VMEM((frames, SPAN), F32),
            pltpu.VMEM((frames, SPAN), BF16),
            pltpu.VMEM((SPAN, SPAN), F32),
        ],
        compiler_params=pltpu.CompilerParams(vmem_limit_bytes=frames * 6 * 2**10 + 8 * 2**20),
        name="chain",
    )(trial_lengths, *everything)
    returned = [back[0]] + [across(back[s], GOING[s]) for s in range(1, heads)]

    *grads, tails = pl.pallas_call(
        unpack_kernel,
        out_shape=[jax.ShapeDtypeStruct((rows, width), BF16)] * 3 + [jax.ShapeDtypeStruct((heads, rows), BF16)],
        in_specs=[SMEM] + [VMEM] * (1 + heads),
        out_specs=[VMEM] * 4,
        compiler_params=pltpu.CompilerParams(vmem_limit_bytes=12 * 2**20),
        name="unpack",
    )(chip, frame_pos.reshape(1, rows), *returned)
    return (*grads, tails.T)


def solution(mesh):
    rows = P(("groups", "ctx"), None)
    return jax.shard_map(
        body,
        mesh=mesh,
        in_specs=(rows, rows, rows, rows, rows, P(("groups", "ctx")), P("groups")),
        out_specs=(rows, rows, rows, rows),
        check_vma=False,
    )
```

```python
import functools

import jax
import jax.numpy as jnp
from jax import lax
from jax.experimental import pallas as pl
from jax.experimental.pallas import tpu as pltpu
from jax.sharding import PartitionSpec as P

SPAN = 128
META = 16
COMING = (0, 1, 2, 6, 7, 4, 5, 3)
GOING = (0, 7, 6, 5, 4, 3, 2, 1)
TOGETHER = 3
F32 = jnp.float32
BF16 = jnp.bfloat16
I32 = jnp.int32
VMEM = pl.BlockSpec(memory_space=pltpu.VMEM)
SMEM = pl.BlockSpec(memory_space=pltpu.SMEM)


def dot(a, b, dims):
    return lax.dot_general(a, b, ((dims[:1], dims[1:]), ((), ())), preferred_element_type=F32)


NN = (1, 0)
NT = (1, 1)
TN = (0, 0)


def iota(shape, dim):
    return lax.broadcasted_iota(I32, shape, dim)


def order(pos):
    rows = pos.shape[1]
    across = jnp.broadcast_to(pos.astype(F32), (rows, rows))
    down = jnp.transpose(across)
    as_row = jnp.sum((down < across).astype(F32), axis=0, keepdims=True)
    as_col = jnp.sum((across < down).astype(F32), axis=1, keepdims=True)
    return as_row.astype(I32), as_col.astype(I32)


def pack_kernel(chip_ref, *refs):
    given, outs, held, built, sems, leaves = refs[:6], refs[6:-9], refs[-9:-3], refs[-3], refs[-2], refs[-1]
    rows = given[0].shape[0]
    heads = len(outs)
    copies = [pltpu.make_async_copy(given[n], held[n], sems.at[n]) for n in range(6)]
    for n in (5, 4, 0, 1, 2, 3):
        copies[n].start()
    chip = chip_ref[0]
    copies[5].wait()
    pos = held[5][...]
    rank, _ = order(pos)
    sort = (rank == iota((rows, rows), 0)).astype(BF16)
    line = iota((META, rows), 0)
    where = jnp.where(line == 1, (pos // SPAN).astype(F32), jnp.where(line == 2, (pos % SPAN + 1).astype(F32), 0.0))
    where = dot(where.astype(BF16), sort, NT)
    copies[4].wait()
    decay = dot(held[4][...], sort, NT)
    for s in range(heads):
        head = chip ^ COMING[s]
        mine = jnp.sum(jnp.where(iota((heads, rows), 0) == head, decay, 0.0), axis=0, keepdims=True)
        built[s, 4 * rows:, :] = jnp.where(line == 0, mine, where).astype(BF16)
    for a in range(4):
        copies[a].wait()
    for s in range(heads):
        head = chip ^ COMING[s]
        at = pl.ds(pl.multiple_of(head * SPAN, SPAN), SPAN)
        together = jnp.concatenate([held[a][:, at] for a in range(4)], axis=1)
        together = dot(sort, together, NN).astype(BF16)
        for a in range(4):
            built[s, a * rows:(a + 1) * rows, :] = together[:, a * SPAN:(a + 1) * SPAN]
        pltpu.make_async_copy(built.at[s], outs[s], leaves.at[s]).start()
    for s in range(heads):
        pltpu.make_async_copy(built.at[s], outs[s], leaves.at[s]).wait()


def segments(position, starts):
    total = jnp.zeros_like(position)
    for start in starts:
        total = total + (position >= start).astype(I32)
    return total


def chain_kernel(heads, lengths_ref, *refs):
    given, answers, scratch = refs[:-heads - 13], refs[-heads - 13:-13], refs[-13:]
    size = min(ref.shape[0] for ref in given)
    blocks = [ref.at[at:at + size] for ref in given for at in range(0, ref.shape[0], size)]
    outs = [answers[GOING.index(s)] for s in COMING]
    sources = len(blocks)
    (hi_ref, lo_ref, win_ref, at_ref, sem, down_ref, cum_ref, chain_ref, gained_ref, weighted_ref,
     pulled_ref, state_ref, tail_ref) = scratch
    rows = (size - META) // 4
    frames = rows * sources
    spans = frames // SPAN
    window = 16 * pl.cdiv(2 * rows // sources, 16) + 16
    tall = cum_ref.shape[0]
    starts = []
    total = jnp.int32(0)
    for t in range(lengths_ref.shape[0]):
        starts.append(total)
        total = total + lengths_ref[t]

    for n, ref in enumerate(blocks):
        meta = ref[4 * rows:, :].astype(F32)
        hi_ref[n:n + 1, :] = meta[1:2]
        lo_ref[n:n + 1, :] = meta[2:3]
    hi = hi_ref[...]
    lane = iota((sources, SPAN), 1)
    count = jnp.zeros((sources, SPAN), F32)
    for b in range(1, spans):
        ahead = jnp.sum((hi < b).astype(F32), axis=1, keepdims=True)
        count = jnp.where(lane == b, ahead, count)
    win_ref[...] = jnp.minimum((count.astype(I32) // 16) * 16, rows - window)
    copy = pltpu.make_async_copy(win_ref, at_ref, sem)
    copy.start()

    spread = []
    hots = []
    for n, ref in enumerate(blocks):
        meta = ref[4 * rows:, :].astype(F32)
        spread.append(jnp.where(meta[1:2] == iota((tall, rows), 0).astype(F32), meta[0:1], 0.0).astype(BF16))
        hots.append((meta[2:3] == (iota((SPAN, rows), 0) + 1).astype(F32)).astype(BF16))
    in_chain = dot(jnp.concatenate(spread, axis=1), jnp.concatenate(hots, axis=1), NT).astype(BF16)
    upper = (iota((SPAN, SPAN), 0) <= iota((SPAN, SPAN), 1)).astype(BF16)
    place = iota((tall, SPAN), 0) * SPAN + iota((tall, SPAN), 1)
    marks = segments(place, starts) - segments(iota((tall, SPAN), 0) * SPAN - 1, starts)
    cum_ref[...] = dot(in_chain, upper, NN) - 128.0 * marks.astype(F32)
    tail_ref[...] = jnp.zeros_like(tail_ref)
    for s, ref in enumerate(outs):
        ref[...] = jnp.zeros_like(ref)
        where = hi_ref[s:s + 1, :] * SPAN + lo_ref[s:s + 1, :] - 1.0
        down_ref[s * rows:(s + 1) * rows, :] = jnp.transpose(jnp.broadcast_to(where, (SPAN, rows)))

    row_i = iota((SPAN, SPAN), 0)
    col_j = iota((SPAN, SPAN), 1)
    per = SPAN // window
    copy.wait()

    def fade(b):
        return jnp.exp(cum_ref[pl.ds(b, 1), SPAN - 1:])

    def first(b, state):
        base = b * SPAN
        at = pl.ds(pl.multiple_of(base, SPAN), SPAN)
        keys = jnp.where(hi_ref[...] == b.astype(F32), lo_ref[...], 0.0)
        chain = jnp.zeros((SPAN, 4 * SPAN), F32)
        for n0 in range(0, sources, 2 * per):
            parts, found = [], []
            for n1 in range(n0, n0 + 2 * per, per):
                row = None
                for n in range(n1, n1 + per):
                    begin = pl.multiple_of(at_ref[n, b], 16)
                    turned = pltpu.roll(keys[n:n + 1], ((n - n1) * window + SPAN - begin) & (SPAN - 1), 1)
                    row = turned if row is None else row + turned
                    found.append(jnp.concatenate(
                        [blocks[n][pl.ds(a * rows + begin, window), :] for a in range(4)], axis=1))
                parts.append(row)
            row = jnp.concatenate(parts, axis=1)
            hot = (row == (iota((SPAN, 2 * per * window), 0) + 1).astype(F32)).astype(BF16)
            chain = chain + dot(hot, jnp.concatenate(found, axis=0), NN)
        chain = chain.astype(BF16)
        chain_ref[at, :] = chain
        q, k, v, g = (chain[:, a * SPAN:(a + 1) * SPAN] for a in range(4))
        cum_j = cum_ref[pl.ds(b, 1), :]
        cum_i = jnp.transpose(jnp.broadcast_to(cum_j, (SPAN, SPAN)))
        last = cum_j[:, SPAN - 1:]
        gap = cum_i - cum_j
        weight = jnp.where(row_i >= col_j, jnp.exp(jnp.minimum(gap, 0.0)), 0.0)
        query_gain = jnp.exp(cum_i)
        key_gain = jnp.exp(last - cum_i)
        key_end = (k.astype(F32) * key_gain).astype(BF16)
        query_start = (q.astype(F32) * query_gain).astype(BF16)
        gained_ref[at, 0:SPAN] = (g.astype(F32) * query_gain).astype(BF16)
        gained_ref[at, SPAN:2 * SPAN] = (v.astype(F32) * key_gain).astype(BF16)
        gained_ref[at, 2 * SPAN:] = key_end
        state_ref[at, :] = state.astype(BF16)
        state = fade(b) * state + dot(key_end, v, TN)
        pulled_ref[at, :] = dot(query_start, g, TN)
        weighted_ref[at, 0:SPAN] = (dot(g, v, NT) * weight).astype(BF16)
        weighted_ref[at, SPAN:] = (dot(q, k, NT) * weight).astype(BF16)
        return state

    def second(b, held):
        base = b * SPAN
        at = pl.ds(pl.multiple_of(base, SPAN), SPAN)
        q, k, v, g = (chain_ref[at, a * SPAN:(a + 1) * SPAN] for a in range(4))
        state = state_ref[at, :]
        grad = held.astype(BF16)
        dq = dot(weighted_ref[at, 0:SPAN], k, NN) + dot(gained_ref[at, 0:SPAN], state, NT)
        dk = dot(weighted_ref[at, 0:SPAN], q, TN) + dot(gained_ref[at, SPAN:2 * SPAN], grad, NT)
        dv = dot(weighted_ref[at, SPAN:], g, TN) + dot(gained_ref[at, 2 * SPAN:], grad, NN)
        term = jnp.sum(q.astype(F32) * dq - k.astype(F32) * dk, axis=1, keepdims=True)
        seg_i = segments(base + row_i, starts)
        seg_j = segments(base + iota((1, SPAN), 1), starts)
        lower = (seg_i == seg_j) & (row_i >= col_j)
        tail_ref[pl.ds(b, 1), :] = jnp.sum(jnp.where(lower, term, 0.0), axis=0, keepdims=True)
        begins = [pl.multiple_of(at_ref[s, b], 16) for s in range(heads)]
        there = jnp.concatenate([down_ref[pl.ds(s * rows + begins[s], window), :] for s in range(heads)], axis=0)
        hot = (there == (base + iota((heads * window, SPAN), 1)).astype(F32)).astype(BF16)
        three = jnp.concatenate([dq.astype(BF16), dk.astype(BF16), dv.astype(BF16)], axis=1)
        back = dot(hot, three, NN).astype(BF16)
        for s in range(heads):
            for a in range(3):
                to = pl.ds(a * rows + begins[s], window)
                outs[s][to, :] += back[s * window:(s + 1) * window, a * SPAN:(a + 1) * SPAN]

        return fade(b) * held + pulled_ref[at, :]

    step = max(1, 256 // sources)
    empty = jnp.zeros((SPAN, SPAN), F32)

    def forward(turn, state):
        for u in range(step):
            state = first(turn * step + u, state)
        return state

    def backward(turn, grad):
        for u in range(step):
            grad = second(spans - 1 - turn * step - u, grad)
        return grad

    lax.fori_loop(0, spans // step, forward, empty)
    lax.fori_loop(0, spans // step, backward, empty)

    firsts = jnp.transpose(tail_ref[...])[0:1, :]
    local = tail_ref[0:tall, :]
    seg_last = segments(iota((tall, SPAN), 0) * SPAN + SPAN - 1, starts)
    seg_first = segments(iota((tall, SPAN), 1) * SPAN, starts)
    later = (iota((tall, SPAN), 1) > iota((tall, SPAN), 0)) & (seg_first == seg_last)
    carry = jnp.sum(jnp.where(later, firsts, 0.0), axis=1, keepdims=True)
    full = local + jnp.where(segments(place, starts) == seg_last, carry, 0.0)
    begins = place == starts[0]
    for start in starts[1:]:
        begins = begins | (place == start)
    tails = jnp.where(begins, 0.0, full).astype(BF16)
    for s in range(heads):
        hot = (lo_ref[s:s + 1, :] == (iota((SPAN, rows), 0) + 1).astype(F32)).astype(BF16)
        found = dot(tails, hot, NN)
        mine = hi_ref[s:s + 1, :] == iota((tall, rows), 0).astype(F32)
        found = jnp.sum(jnp.where(mine, found, 0.0), axis=0, keepdims=True)
        outs[s][3 * rows:, :] = jnp.broadcast_to(found, (META, rows)).astype(BF16)


def join_kernel(*refs):
    size = refs[0].shape[0]
    for n, ref in enumerate(refs[:-1]):
        refs[-1][n * size:(n + 1) * size, :] = ref[...]


def unpack_kernel(chip_ref, pos_ref, *refs):
    heads = len(refs) - 4
    blocks, outs = refs[:heads], refs[heads:]
    rows = outs[0].shape[0]
    chip = chip_ref[0]
    _, rank = order(pos_ref[...])
    loose = (rank == iota((rows, rows), 1)).astype(BF16)
    line = iota((META, rows), 0)
    tails = jnp.zeros((META, rows), F32)
    for s in range(heads):
        head = chip ^ GOING[s]
        at = pl.ds(pl.multiple_of(head * SPAN, SPAN), SPAN)
        together = jnp.concatenate([blocks[s][a * rows:(a + 1) * rows, :] for a in range(3)], axis=1)
        together = dot(loose, together, NN).astype(BF16)
        for a in range(3):
            outs[a][:, at] = together[:, a * SPAN:(a + 1) * SPAN]
        tails = jnp.where(line == head, blocks[s][3 * rows:, :].astype(F32), tails)
    outs[3][...] = dot(tails.astype(BF16), loose, NT)[:heads].astype(BF16)


def body(queries, keys, values, out_grad, log_decay, frame_pos, trial_lengths):
    rows, width = queries.shape
    heads = log_decay.shape[1]
    peers = lax.axis_size("ctx")
    cores = peers // heads
    frames = rows * peers
    spans = frames // SPAN
    chip = (lax.axis_index("ctx") // cores).astype(I32).reshape(1)

    def across(x, s):
        return lax.ppermute(x, "ctx", [(p, p ^ (s * cores)) for p in range(peers)])

    def beside(x, t):
        return lax.ppermute(x, "ctx", [(p, p ^ t) for p in range(peers)])

    packets = pl.pallas_call(
        pack_kernel,
        out_shape=[jax.ShapeDtypeStruct((4 * rows + META, SPAN), BF16)] * heads,
        in_specs=[SMEM] + [pl.BlockSpec(memory_space=pltpu.HBM)] * 6,
        out_specs=[pl.BlockSpec(memory_space=pltpu.HBM)] * heads,
        scratch_shapes=[pltpu.VMEM((rows, width), BF16)] * 4
        + [pltpu.VMEM((heads, rows), BF16), pltpu.VMEM((1, rows), I32), pltpu.VMEM((heads, 4 * rows + META, SPAN), BF16)]
        + [pltpu.SemaphoreType.DMA((6,)), pltpu.SemaphoreType.DMA((heads,))],
        compiler_params=pltpu.CompilerParams(vmem_limit_bytes=60 * 2**20),
        name="pack",
    )(chip, queries, keys, values, out_grad, log_decay.T, frame_pos.reshape(1, rows))
    got = [packets[0]] + [across(packets[s], COMING[s]) for s in range(1, heads)]
    size = 4 * rows + META
    joined = pl.pallas_call(
        join_kernel,
        out_shape=jax.ShapeDtypeStruct((TOGETHER * size, SPAN), BF16),
        in_specs=[VMEM] * TOGETHER,
        out_specs=VMEM,
        compiler_params=pltpu.CompilerParams(vmem_limit_bytes=4 * 2**20),
        cost_estimate=pl.CostEstimate(flops=2**30, bytes_accessed=2**18, transcendentals=0),
        name="join",
    )(*got[:TOGETHER])
    got = [joined, *got[TOGETHER:]]
    everything = list(got)
    for t in range(1, cores):
        everything += [beside(x, t) for x in got]

    tall = max(META, spans)
    back = pl.pallas_call(
        functools.partial(chain_kernel, heads),
        out_shape=[jax.ShapeDtypeStruct((3 * rows + META, SPAN), BF16)] * heads,
        in_specs=[SMEM] + [VMEM] * len(everything),
        out_specs=[VMEM] * heads,
        scratch_shapes=[
            pltpu.VMEM((peers, SPAN), F32),
            pltpu.VMEM((peers, SPAN), F32),
            pltpu.VMEM((peers, SPAN), I32),
            pltpu.SMEM((peers, SPAN), I32),
            pltpu.SemaphoreType.DMA,
            pltpu.VMEM((heads * rows, SPAN), F32),
            pltpu.VMEM((tall, SPAN), F32),
            pltpu.VMEM((frames, 4 * SPAN), BF16),
            pltpu.VMEM((frames, 3 * SPAN), BF16),
            pltpu.VMEM((frames, 2 * SPAN), BF16),
            pltpu.VMEM((frames, SPAN), F32),
            pltpu.VMEM((frames, SPAN), BF16),
            pltpu.VMEM((SPAN, SPAN), F32),
        ],
        compiler_params=pltpu.CompilerParams(vmem_limit_bytes=frames * 6 * 2**10 + 8 * 2**20),
        name="chain",
    )(trial_lengths, *everything)
    returned = [back[0]] + [across(back[s], GOING[s]) for s in range(1, heads)]

    *grads, tails = pl.pallas_call(
        unpack_kernel,
        out_shape=[jax.ShapeDtypeStruct((rows, width), BF16)] * 3 + [jax.ShapeDtypeStruct((heads, rows), BF16)],
        in_specs=[SMEM] + [VMEM] * (1 + heads),
        out_specs=[VMEM] * 4,
        compiler_params=pltpu.CompilerParams(vmem_limit_bytes=12 * 2**20),
        name="unpack",
    )(chip, frame_pos.reshape(1, rows), *returned)
    return (*grads, tails.T)


def solution(mesh):
    rows = P(("groups", "ctx"), None)
    return jax.shard_map(
        body,
        mesh=mesh,
        in_specs=(rows, rows, rows, rows, rows, P(("groups", "ctx")), P("groups")),
        out_specs=(rows, rows, rows, rows),
        check_vma=False,
    )
```

```python
import functools

import jax
import jax.numpy as jnp
from jax import lax
from jax.experimental import pallas as pl
from jax.experimental.pallas import tpu as pltpu
from jax.sharding import PartitionSpec as P

SPAN = 128
META = 16
COMING = (0, 1, 2, 6, 7, 4, 5, 3)
GOING = (0, 7, 6, 5, 4, 3, 2, 1)
TOGETHER = 3
F32 = jnp.float32
BF16 = jnp.bfloat16
I32 = jnp.int32
VMEM = pl.BlockSpec(memory_space=pltpu.VMEM)
SMEM = pl.BlockSpec(memory_space=pltpu.SMEM)


def dot(a, b, dims):
    return lax.dot_general(a, b, ((dims[:1], dims[1:]), ((), ())), preferred_element_type=F32)


NN = (1, 0)
NT = (1, 1)
TN = (0, 0)


def iota(shape, dim):
    return lax.broadcasted_iota(I32, shape, dim)


def order(pos):
    rows = pos.shape[1]
    across = jnp.broadcast_to(pos.astype(F32), (rows, rows))
    down = jnp.transpose(across)
    as_row = jnp.sum((down < across).astype(F32), axis=0, keepdims=True)
    as_col = jnp.sum((across < down).astype(F32), axis=1, keepdims=True)
    return as_row.astype(I32), as_col.astype(I32)


def pack_kernel(chip_ref, *refs):
    given, outs, held, built, sems, leaves = refs[:6], refs[6:-9], refs[-9:-3], refs[-3], refs[-2], refs[-1]
    rows = given[0].shape[0]
    heads = len(outs)
    copies = [pltpu.make_async_copy(given[n], held[n], sems.at[n]) for n in range(6)]
    for n in (5, 4, 0, 1, 2, 3):
        copies[n].start()
    chip = chip_ref[0]
    copies[5].wait()
    pos = held[5][...]
    rank, _ = order(pos)
    sort = (rank == iota((rows, rows), 0)).astype(BF16)
    line = iota((META, rows), 0)
    where = jnp.where(line == 1, (pos // SPAN).astype(F32), jnp.where(line == 2, (pos % SPAN + 1).astype(F32), 0.0))
    where = dot(where.astype(BF16), sort, NT)
    copies[4].wait()
    decay = dot(held[4][...], sort, NT)
    for s in range(heads):
        head = chip ^ COMING[s]
        mine = jnp.sum(jnp.where(iota((heads, rows), 0) == head, decay, 0.0), axis=0, keepdims=True)
        built[s, 4 * rows:, :] = jnp.where(line == 0, mine, where).astype(BF16)
    for a in range(4):
        copies[a].wait()
    for s in range(heads):
        head = chip ^ COMING[s]
        at = pl.ds(pl.multiple_of(head * SPAN, SPAN), SPAN)
        together = jnp.concatenate([held[a][:, at] for a in range(4)], axis=1)
        together = dot(sort, together, NN).astype(BF16)
        for a in range(4):
            built[s, a * rows:(a + 1) * rows, :] = together[:, a * SPAN:(a + 1) * SPAN]
        pltpu.make_async_copy(built.at[s], outs[s], leaves.at[s]).start()
    for s in range(heads):
        pltpu.make_async_copy(built.at[s], outs[s], leaves.at[s]).wait()


def segments(position, starts):
    total = jnp.zeros_like(position)
    for start in starts:
        total = total + (position >= start).astype(I32)
    return total


def chain_kernel(heads, lengths_ref, *refs):
    given, answers, scratch = refs[:-heads - 13], refs[-heads - 13:-13], refs[-13:]
    size = min(ref.shape[0] for ref in given)
    blocks = [ref.at[at:at + size] for ref in given for at in range(0, ref.shape[0], size)]
    outs = [answers[GOING.index(s)] for s in COMING]
    sources = len(blocks)
    (hi_ref, lo_ref, win_ref, at_ref, sem, down_ref, cum_ref, chain_ref, gained_ref, weighted_ref,
     pulled_ref, state_ref, tail_ref) = scratch
    rows = (size - META) // 4
    frames = rows * sources
    spans = frames // SPAN
    window = 16 * pl.cdiv(2 * rows // sources, 16) + 16
    tall = cum_ref.shape[0]
    starts = []
    total = jnp.int32(0)
    for t in range(lengths_ref.shape[0]):
        starts.append(total)
        total = total + lengths_ref[t]

    for n, ref in enumerate(blocks):
        meta = ref[4 * rows:, :].astype(F32)
        hi_ref[n:n + 1, :] = meta[1:2]
        lo_ref[n:n + 1, :] = meta[2:3]
    hi = hi_ref[...]
    lane = iota((sources, SPAN), 1)
    count = jnp.zeros((sources, SPAN), F32)
    for b in range(1, spans):
        ahead = jnp.sum((hi < b).astype(F32), axis=1, keepdims=True)
        count = jnp.where(lane == b, ahead, count)
    win_ref[...] = jnp.minimum((count.astype(I32) // 16) * 16, rows - window)
    copy = pltpu.make_async_copy(win_ref, at_ref, sem)
    copy.start()

    spread = []
    hots = []
    for n, ref in enumerate(blocks):
        meta = ref[4 * rows:, :].astype(F32)
        spread.append(jnp.where(meta[1:2] == iota((tall, rows), 0).astype(F32), meta[0:1], 0.0).astype(BF16))
        hots.append((meta[2:3] == (iota((SPAN, rows), 0) + 1).astype(F32)).astype(BF16))
    in_chain = dot(jnp.concatenate(spread, axis=1), jnp.concatenate(hots, axis=1), NT).astype(BF16)
    upper = (iota((SPAN, SPAN), 0) <= iota((SPAN, SPAN), 1)).astype(BF16)
    place = iota((tall, SPAN), 0) * SPAN + iota((tall, SPAN), 1)
    marks = segments(place, starts) - segments(iota((tall, SPAN), 0) * SPAN - 1, starts)
    cum_ref[...] = dot(in_chain, upper, NN) - 128.0 * marks.astype(F32)
    tail_ref[...] = jnp.zeros_like(tail_ref)
    for s, ref in enumerate(outs):
        ref[...] = jnp.zeros_like(ref)
        where = hi_ref[s:s + 1, :] * SPAN + lo_ref[s:s + 1, :] - 1.0
        down_ref[s * rows:(s + 1) * rows, :] = jnp.transpose(jnp.broadcast_to(where, (SPAN, rows)))

    row_i = iota((SPAN, SPAN), 0)
    col_j = iota((SPAN, SPAN), 1)
    per = SPAN // window
    copy.wait()

    def fade(b):
        return jnp.exp(cum_ref[pl.ds(b, 1), SPAN - 1:])

    def first(b, state):
        base = b * SPAN
        at = pl.ds(pl.multiple_of(base, SPAN), SPAN)
        keys = jnp.where(hi_ref[...] == b.astype(F32), lo_ref[...], 0.0)
        chain = jnp.zeros((SPAN, 4 * SPAN), F32)
        for n0 in range(0, sources, 2 * per):
            parts, found = [], []
            for n1 in range(n0, n0 + 2 * per, per):
                row = None
                for n in range(n1, n1 + per):
                    begin = pl.multiple_of(at_ref[n, b], 16)
                    turned = pltpu.roll(keys[n:n + 1], ((n - n1) * window + SPAN - begin) & (SPAN - 1), 1)
                    row = turned if row is None else row + turned
                    found.append(jnp.concatenate(
                        [blocks[n][pl.ds(a * rows + begin, window), :] for a in range(4)], axis=1))
                parts.append(row)
            row = jnp.concatenate(parts, axis=1)
            hot = (row == (iota((SPAN, 2 * per * window), 0) + 1).astype(F32)).astype(BF16)
            chain = chain + dot(hot, jnp.concatenate(found, axis=0), NN)
        chain = chain.astype(BF16)
        chain_ref[at, :] = chain
        q, k, v, g = (chain[:, a * SPAN:(a + 1) * SPAN] for a in range(4))
        cum_j = cum_ref[pl.ds(b, 1), :]
        cum_i = jnp.transpose(jnp.broadcast_to(cum_j, (SPAN, SPAN)))
        last = cum_j[:, SPAN - 1:]
        gap = cum_i - cum_j
        weight = jnp.where(row_i >= col_j, jnp.exp(jnp.minimum(gap, 0.0)), 0.0)
        query_gain = jnp.exp(cum_i)
        key_gain = jnp.exp(last - cum_i)
        key_end = (k.astype(F32) * key_gain).astype(BF16)
        query_start = (q.astype(F32) * query_gain).astype(BF16)
        gained_ref[at, 0:SPAN] = (g.astype(F32) * query_gain).astype(BF16)
        gained_ref[at, SPAN:2 * SPAN] = (v.astype(F32) * key_gain).astype(BF16)
        gained_ref[at, 2 * SPAN:] = key_end
        state_ref[at, :] = state.astype(BF16)
        state = fade(b) * state + dot(key_end, v, TN)
        pulled_ref[at, :] = dot(query_start, g, TN)
        weighted_ref[at, 0:SPAN] = (dot(g, v, NT) * weight).astype(BF16)
        weighted_ref[at, SPAN:] = (dot(q, k, NT) * weight).astype(BF16)
        return state

    def second(b, held):
        base = b * SPAN
        at = pl.ds(pl.multiple_of(base, SPAN), SPAN)
        q, k, v, g = (chain_ref[at, a * SPAN:(a + 1) * SPAN] for a in range(4))
        state = state_ref[at, :]
        grad = held.astype(BF16)
        dq = dot(weighted_ref[at, 0:SPAN], k, NN) + dot(gained_ref[at, 0:SPAN], state, NT)
        dk = dot(weighted_ref[at, 0:SPAN], q, TN) + dot(gained_ref[at, SPAN:2 * SPAN], grad, NT)
        dv = dot(weighted_ref[at, SPAN:], g, TN) + dot(gained_ref[at, 2 * SPAN:], grad, NN)
        term = jnp.sum(q.astype(F32) * dq - k.astype(F32) * dk, axis=1, keepdims=True)
        seg_i = segments(base + row_i, starts)
        seg_j = segments(base + iota((1, SPAN), 1), starts)
        lower = (seg_i == seg_j) & (row_i >= col_j)
        tail_ref[pl.ds(b, 1), :] = jnp.sum(jnp.where(lower, term, 0.0), axis=0, keepdims=True)
        begins = [pl.multiple_of(at_ref[s, b], 16) for s in range(heads)]
        there = jnp.concatenate([down_ref[pl.ds(s * rows + begins[s], window), :] for s in range(heads)], axis=0)
        hot = (there == (base + iota((heads * window, SPAN), 1)).astype(F32)).astype(BF16)
        three = jnp.concatenate([dq.astype(BF16), dk.astype(BF16), dv.astype(BF16)], axis=1)
        back = dot(hot, three, NN).astype(BF16)
        for s in range(heads):
            for a in range(3):
                to = pl.ds(a * rows + begins[s], window)
                outs[s][to, :] += back[s * window:(s + 1) * window, a * SPAN:(a + 1) * SPAN]

        return fade(b) * held + pulled_ref[at, :]

    step = max(1, 256 // sources)
    empty = jnp.zeros((SPAN, SPAN), F32)

    def forward(turn, state):
        for u in range(step):
            state = first(turn * step + u, state)
        return state

    def backward(turn, grad):
        for u in range(step):
            grad = second(spans - 1 - turn * step - u, grad)
        return grad

    lax.fori_loop(0, spans // step, forward, empty)
    lax.fori_loop(0, spans // step, backward, empty)

    firsts = jnp.transpose(tail_ref[...])[0:1, :]
    local = tail_ref[0:tall, :]
    seg_last = segments(iota((tall, SPAN), 0) * SPAN + SPAN - 1, starts)
    seg_first = segments(iota((tall, SPAN), 1) * SPAN, starts)
    later = (iota((tall, SPAN), 1) > iota((tall, SPAN), 0)) & (seg_first == seg_last)
    carry = jnp.sum(jnp.where(later, firsts, 0.0), axis=1, keepdims=True)
    full = local + jnp.where(segments(place, starts) == seg_last, carry, 0.0)
    begins = place == starts[0]
    for start in starts[1:]:
        begins = begins | (place == start)
    tails = jnp.where(begins, 0.0, full).astype(BF16)
    for s in range(heads):
        hot = (lo_ref[s:s + 1, :] == (iota((SPAN, rows), 0) + 1).astype(F32)).astype(BF16)
        found = dot(tails, hot, NN)
        mine = hi_ref[s:s + 1, :] == iota((tall, rows), 0).astype(F32)
        found = jnp.sum(jnp.where(mine, found, 0.0), axis=0, keepdims=True)
        outs[s][3 * rows:, :] = jnp.broadcast_to(found, (META, rows)).astype(BF16)


def join_kernel(pos_ref, *refs):
    blocks, joined_ref, loose_ref = refs[:-2], refs[-2], refs[-1]
    size = blocks[0].shape[0]
    rows = pos_ref.shape[1]
    for n, ref in enumerate(blocks):
        joined_ref[n * size:(n + 1) * size, :] = ref[...]
    _, rank = order(pos_ref[...])
    loose_ref[...] = (rank == iota((rows, rows), 1)).astype(BF16)


def unpack_kernel(chip_ref, loose_ref, *refs):
    heads = len(refs) - 4
    blocks, outs = refs[:heads], refs[heads:]
    rows = outs[0].shape[0]
    chip = chip_ref[0]
    loose = loose_ref[...]
    line = iota((META, rows), 0)
    tails = jnp.zeros((META, rows), F32)
    for s in range(heads):
        head = chip ^ GOING[s]
        at = pl.ds(pl.multiple_of(head * SPAN, SPAN), SPAN)
        together = jnp.concatenate([blocks[s][a * rows:(a + 1) * rows, :] for a in range(3)], axis=1)
        together = dot(loose, together, NN).astype(BF16)
        for a in range(3):
            outs[a][:, at] = together[:, a * SPAN:(a + 1) * SPAN]
        tails = jnp.where(line == head, blocks[s][3 * rows:, :].astype(F32), tails)
    outs[3][...] = dot(tails.astype(BF16), loose, NT)[:heads].astype(BF16)


def body(queries, keys, values, out_grad, log_decay, frame_pos, trial_lengths):
    rows, width = queries.shape
    heads = log_decay.shape[1]
    peers = lax.axis_size("ctx")
    cores = peers // heads
    frames = rows * peers
    spans = frames // SPAN
    chip = (lax.axis_index("ctx") // cores).astype(I32).reshape(1)

    def across(x, s):
        return lax.ppermute(x, "ctx", [(p, p ^ (s * cores)) for p in range(peers)])

    def beside(x, t):
        return lax.ppermute(x, "ctx", [(p, p ^ t) for p in range(peers)])

    packets = pl.pallas_call(
        pack_kernel,
        out_shape=[jax.ShapeDtypeStruct((4 * rows + META, SPAN), BF16)] * heads,
        in_specs=[SMEM] + [pl.BlockSpec(memory_space=pltpu.HBM)] * 6,
        out_specs=[pl.BlockSpec(memory_space=pltpu.HBM)] * heads,
        scratch_shapes=[pltpu.VMEM((rows, width), BF16)] * 4
        + [pltpu.VMEM((heads, rows), BF16), pltpu.VMEM((1, rows), I32), pltpu.VMEM((heads, 4 * rows + META, SPAN), BF16)]
        + [pltpu.SemaphoreType.DMA((6,)), pltpu.SemaphoreType.DMA((heads,))],
        compiler_params=pltpu.CompilerParams(vmem_limit_bytes=60 * 2**20),
        name="pack",
    )(chip, queries, keys, values, out_grad, log_decay.T, frame_pos.reshape(1, rows))
    got = [packets[0]] + [across(packets[s], COMING[s]) for s in range(1, heads)]
    size = 4 * rows + META
    joined, loose = pl.pallas_call(
        join_kernel,
        out_shape=[jax.ShapeDtypeStruct((TOGETHER * size, SPAN), BF16), jax.ShapeDtypeStruct((rows, rows), BF16)],
        in_specs=[VMEM] * (1 + TOGETHER),
        out_specs=[VMEM] * 2,
        compiler_params=pltpu.CompilerParams(vmem_limit_bytes=4 * 2**20),
        cost_estimate=pl.CostEstimate(flops=2**30, bytes_accessed=2**18, transcendentals=0),
        name="join",
    )(frame_pos.reshape(1, rows), *got[:TOGETHER])
    got = [joined, *got[TOGETHER:]]
    everything = list(got)
    for t in range(1, cores):
        everything += [beside(x, t) for x in got]

    tall = max(META, spans)
    back = pl.pallas_call(
        functools.partial(chain_kernel, heads),
        out_shape=[jax.ShapeDtypeStruct((3 * rows + META, SPAN), BF16)] * heads,
        in_specs=[SMEM] + [VMEM] * len(everything),
        out_specs=[VMEM] * heads,
        scratch_shapes=[
            pltpu.VMEM((peers, SPAN), F32),
            pltpu.VMEM((peers, SPAN), F32),
            pltpu.VMEM((peers, SPAN), I32),
            pltpu.SMEM((peers, SPAN), I32),
            pltpu.SemaphoreType.DMA,
            pltpu.VMEM((heads * rows, SPAN), F32),
            pltpu.VMEM((tall, SPAN), F32),
            pltpu.VMEM((frames, 4 * SPAN), BF16),
            pltpu.VMEM((frames, 3 * SPAN), BF16),
            pltpu.VMEM((frames, 2 * SPAN), BF16),
            pltpu.VMEM((frames, SPAN), F32),
            pltpu.VMEM((frames, SPAN), BF16),
            pltpu.VMEM((SPAN, SPAN), F32),
        ],
        compiler_params=pltpu.CompilerParams(vmem_limit_bytes=frames * 6 * 2**10 + 8 * 2**20),
        name="chain",
    )(trial_lengths, *everything)
    returned = [back[0]] + [across(back[s], GOING[s]) for s in range(1, heads)]

    *grads, tails = pl.pallas_call(
        unpack_kernel,
        out_shape=[jax.ShapeDtypeStruct((rows, width), BF16)] * 3 + [jax.ShapeDtypeStruct((heads, rows), BF16)],
        in_specs=[SMEM] + [VMEM] * (1 + heads),
        out_specs=[VMEM] * 4,
        compiler_params=pltpu.CompilerParams(vmem_limit_bytes=12 * 2**20),
        name="unpack",
    )(chip, loose, *returned)
    return (*grads, tails.T)


def solution(mesh):
    rows = P(("groups", "ctx"), None)
    return jax.shard_map(
        body,
        mesh=mesh,
        in_specs=(rows, rows, rows, rows, rows, P(("groups", "ctx")), P("groups")),
        out_specs=(rows, rows, rows, rows),
        check_vma=False,
    )
```
